512 devices in a mesh: seq: 64 (over x, z, core), exp: 8 (over y).
Axes of the slice: x: 4, y: 8, z: 8, core: 2. Of those that a mesh axis runs over, the one named last changes fastest.
Arguments:
- residual: bfloat16 [8, 2048, 2048], P('exp', 'seq'), may hold values from -6 to 6
- queries: bfloat16 [8, 2048, 1024], P('exp', 'seq'), may hold values from -8 to 8
- keys: bfloat16 [8, 2048, 1024], P('exp', 'seq'), may hold values from -6 to 6
- values: bfloat16 [8, 2048, 1024], P('exp', 'seq'), may hold values from -6 to 6
- block_mask: int32 [8, 16, 16], P('exp'), may hold values 0 or 1
- out_weight: bfloat16 [1024, 2048], P(None, 'exp'), may hold values from -0.1875 to 0.1875
- norm_gain: float32 [2048], replicated, may hold values from 0.1 to 1.9
- router: bfloat16 [2048, 64], replicated, may hold values from -0.125 to 0.125
- route_ids: int32 [8, 2048, 2], P('exp', 'seq'), may hold values from 0 to 63, all different within a row; in each aligned block of 32 rows (0 to 31, 32 to 63, ..., all dimensions but the last counted through in order) at most 2 rows name the same one
- w_gate: bfloat16 [64, 2048, 1408], P('seq', None, 'exp'), may hold values from -0.125 to 0.125
- w_up: bfloat16 [64, 2048, 1408], P('seq', None, 'exp'), may hold values from -0.125 to 0.125
- w_down: bfloat16 [64, 1408, 2048], P('seq', 'exp'), may hold values from -0.15625 to 0.15625
Outputs:
- attended: bfloat16 [8, 2048, 1024], P('exp', 'seq')
- mixed: bfloat16 [8, 2048, 2048], P('exp', 'seq')
The draws below stay inside these ranges and needn't reach their ends.
Inputs may be any that keep to these rules, and one draw needn't show every extreme that they name: `route_ids`: each event names two different experts; among the events of one device block no expert is named more than 2 times, a bound that some block reaches.
All inputs are finite; a program needn't handle non-finite values. No bound on the sum of `block_mask` on one device may be relied on, other than what follows from the above.
Results may differ from the reference program's by a relative error of at most 0.013.
Values may be sent and summed in bfloat16 or wider, within the bound.
No kernel may reach another device: no remote copies, remote signals or barrier semaphores. Data moves between devices by JAX's collectives and lax.ppermute only.
A program may use at most 64 MiB of HBM per device.

```python
import math
import jax
import jax.numpy as jnp
import numpy as np
from jax import lax

D = 2048
HEADS = 8
HEAD = 128
HD = 1024
FF = 1408
EXPERTS = 64
CAP = 2
BLOCK = 128
TOK_DEV = 32
STREAMS = 8
LEN = 2048
NB = 16
N_SEQ = 64
N_EXP = 8


def draw_queries(key, part):
    key = jax.random.fold_in(key, 11)
    result = jnp.clip(jax.random.normal(key, (STREAMS, LEN, HD), jnp.float32), -6.0, 6.0)
    return result.astype(jnp.bfloat16)


def draw_keys(key, part):
    key = jax.random.fold_in(key, 13)
    result = jnp.clip(jax.random.normal(key, (STREAMS, LEN, HD), jnp.float32), -6.0, 6.0)
    return result.astype(jnp.bfloat16)


def set_ends(values, key, least, top_value):
    longest = values.shape.index(max(values.shape))
    spots = []
    for shift in (0, 1):
        where = [jax.random.randint(jax.random.fold_in(key, axis), (), 0, length) for axis, length in enumerate(values.shape)]
        where[longest] = (where[longest] + shift) % values.shape[longest]
        spots.append(tuple(where))
    return values.at[spots[0]].set(least).at[spots[1]].set(top_value)


def levels(own_key, extent, shards, least, largest):
    level, own = 1.0, jax.random.fold_in(own_key, 6)
    for dim, blocks in shards:
        steps = jnp.exp(jax.random.uniform(jax.random.fold_in(own, dim), (blocks,), jnp.float32, least / len(shards), largest / len(shards)))
        level = level * jnp.repeat(steps, extent[dim] // blocks).reshape([-1 if axis == dim else 1 for axis in range(len(extent))])
    return level


def routed_block(stream_key, own, number, rows, count, top, reach, skew):
    ranking = jax.random.permutation(stream_key, count)
    crowded, common = shares(count, rows * top, reach, skew, True), shares(count, rows * top, reach, skew, False)
    places = jnp.arange(count)

    def named(tallies, rotation):
        used = int((tallies > 0).sum())
        fixed = max(1, used // 4)
        passed = fixed + (places - fixed + rotation * (used - fixed)) % max(1, count - fixed)
        return jnp.zeros((count,), jnp.int32).at[ranking[jnp.where(places < fixed, places, passed)]].set(jnp.asarray(tallies, jnp.int32))

    tallies = jnp.where(number % 4 == 0, named(crowded, number // 4), named(common, number - number // 4 - 1))
    mixed = jax.random.permutation(jax.random.fold_in(own, 3), count)
    source_of, taker = mixed[0:count // 2 * 2:2], mixed[1:count // 2 * 2:2]
    room = jnp.minimum(tallies[source_of] - 1, reach - tallies[taker]) // 2
    room = jnp.where((source_of == ranking[0]) | (taker == ranking[0]) | (tallies[taker] == 0), 0, jnp.maximum(room, 0))
    passed = jax.random.randint(jax.random.fold_in(own, 4), (count // 2,), 0, 1 << 20) % (room + 1)
    tallies = tallies.at[source_of].add(-passed).at[taker].add(passed)
    labels = jnp.searchsorted(jnp.cumsum(tallies), jnp.arange(rows * top), side="right").astype(jnp.int32)
    listing = labels.reshape(top, rows).T
    listing = listing[jax.random.permutation(jax.random.fold_in(own, 1), rows)]
    rotation = jax.random.randint(jax.random.fold_in(own, 2), (rows, 1), 0, top)
    return jnp.take_along_axis(listing, (jnp.arange(top)[None, :] + rotation) % top, axis=1)


def shares(number_of, total, limit, slope, full):
    loads = [(1 << 20) // math.isqrt(rank ** slope) + 1 for rank in range(1, number_of + 1)]
    largest = limit if full else min(limit, max(-(-total // number_of), total * loads[0] // sum(loads)))
    least = 1 if total - largest >= number_of - 1 else 0
    counts, spare = [largest] + [least] * (number_of - 1), total - largest - least * (number_of - 1)
    while spare > 0:
        candidates = [i for i in range(1, number_of) if counts[i] < largest] or [i for i in range(1, number_of) if counts[i] < limit]
        whole, budget = sum([loads[i] for i in candidates]), spare
        for i in candidates:
            extra = min(limit - counts[i], max(1, budget * loads[i] // whole), spare)
            counts[i] = counts[i] + extra
            spare = spare - extra
    return np.array(counts)


def centred(key, extent, deviation, limit, split=(), kind=jnp.bfloat16):
    array = jax.random.normal(key, extent, jnp.float32) * deviation
    if len(split) > 0:
        array = levels(key, extent, split, -0.22, 0.18) * array
    return jnp.clip(array, min=-limit, max=limit).astype(kind)


def setup_inputs(seed: int = 0) -> dict:
    key_list = jax.random.split(jax.random.key(seed), 13)
    residual = centred(key_list[0], (STREAMS, LEN, D), 1.0, 6.0, ((0, 8), (1, 64)))
    queries = draw_queries(jax.random.fold_in(key_list[12], 71), 0)
    keys = draw_keys(jax.random.fold_in(key_list[12], 71), 0)
    values = centred(key_list[3], (STREAMS, LEN, HD), 1.0, 6.0, ((0, 8), (1, 64)))
    block_mask = set_ends((jax.random.randint(key_list[4], (STREAMS, NB, NB), 0, 2) < 1).astype(jnp.int32), jax.random.fold_in(key_list[4], 1), 0, 1)
    out_weight = centred(key_list[5], (HD, D), HD ** -0.5, 0.1875, ((1, 8),))
    norm_gain = jnp.clip(1.0 + 0.18 * jax.random.normal(key_list[6], (D,), jnp.float32), 0.1, 1.9)
    router = centred(key_list[7], (D, EXPERTS), D ** -0.5, 0.125)
    route_ids_keys = jax.random.split(jax.random.fold_in(key_list[8], 1), STREAMS * LEN // TOK_DEV)
    route_ids_turns = jax.random.permutation(jax.random.fold_in(key_list[8], 3), STREAMS * LEN // TOK_DEV)
    route_ids = jax.vmap(lambda own, number: routed_block(jax.random.fold_in(key_list[8], 2), own, number, TOK_DEV, EXPERTS, 2, CAP, 2))(route_ids_keys, route_ids_turns).reshape((STREAMS, LEN, 2))
    w_gate = centred(key_list[9], (EXPERTS, D, FF), D ** -0.5, 0.125, ((0, 64), (2, 8)))
    w_up = centred(key_list[10], (EXPERTS, D, FF), D ** -0.5, 0.125, ((0, 64), (2, 8)))
    w_down = centred(key_list[11], (EXPERTS, FF, D), FF ** -0.5, 0.15625, ((0, 64), (1, 8)))
    return {"residual": residual, "queries": queries, "keys": keys, "values": values, "block_mask": block_mask, "out_weight": out_weight, "norm_gain": norm_gain, "router": router, "route_ids": route_ids, "w_gate": w_gate, "w_up": w_up, "w_down": w_down}


def attend_stream(args):
    query_s, key_s, value_s, mask_s = args
    live = (mask_s > 0) | jnp.eye(NB, dtype=bool)
    widened = jnp.repeat(jnp.repeat(live, BLOCK, axis=0), BLOCK, axis=1)
    positions = jnp.arange(LEN)
    allowed = widened & (positions[None, :] <= positions[:, None])
    query_h = query_s.reshape(LEN, HEADS, HEAD).transpose(1, 0, 2)
    key_h = key_s.reshape(LEN, HEADS, HEAD).transpose(1, 0, 2)
    value_h = value_s.reshape(LEN, HEADS, HEAD).transpose(1, 0, 2)
    scale_factor = HEAD ** (-0.5)

    def one_head(inner):
        query_one, key_one, value_one = inner
        scores = jnp.dot(query_one, key_one.T, preferred_element_type=jnp.float32) * scale_factor
        scores = jnp.where(allowed, scores, -1e+30)
        highest = lax.optimization_barrier(jnp.max(scores, axis=1, keepdims=True))
        weights = jnp.where(allowed, jnp.exp(scores - highest), 0.0)
        total = lax.optimization_barrier(jnp.sum(weights, axis=1, keepdims=True))
        return jnp.dot(weights.astype(jnp.bfloat16), value_one, preferred_element_type=jnp.float32) / total
    heads_out = lax.map(one_head, (query_h, key_h, value_h))
    return heads_out.transpose(1, 0, 2).reshape(LEN, HD).astype(jnp.bfloat16)

def reference(residual, queries, keys, values, block_mask, out_weight, norm_gain, router, route_ids, w_gate, w_up, w_down):
    attended = lax.map(attend_stream, (queries, keys, values, block_mask))
    projected = jnp.dot(attended.reshape(-1, HD), out_weight, preferred_element_type=jnp.float32)
    projected = projected.astype(jnp.bfloat16).reshape(STREAMS, LEN, D)
    hidden_one = residual.astype(jnp.float32) + projected.astype(jnp.float32)
    meansq = lax.optimization_barrier(jnp.mean(hidden_one * hidden_one, axis=-1, keepdims=True))
    normed = (hidden_one * lax.rsqrt(meansq + 1e-06) * norm_gain).astype(jnp.bfloat16)
    logits = jnp.dot(normed.reshape(-1, D), router, preferred_element_type=jnp.float32)
    logits = logits.reshape(STREAMS, LEN, EXPERTS)
    chosen = jnp.take_along_axis(logits, route_ids, axis=2)
    first_gate = jax.nn.sigmoid(chosen[..., 0] - chosen[..., 1])
    gates = jnp.stack([first_gate, 1.0 - first_gate], axis=-1)
    grouped = route_ids.reshape(STREAMS, N_SEQ, 2 * TOK_DEV)
    onehot = (grouped[..., None] == jnp.arange(EXPERTS, dtype=jnp.int32)).astype(jnp.int32)
    earlier = jnp.cumsum(onehot, axis=2) - onehot
    slots = lax.optimization_barrier(jnp.sum(earlier * onehot, axis=-1)).astype(jnp.int32)
    rows = jnp.repeat(normed.reshape(STREAMS, N_SEQ, TOK_DEV, D), 2, axis=2)
    stream_idx = jnp.arange(STREAMS, dtype=jnp.int32)[:, None, None]
    device_idx = jnp.arange(N_SEQ, dtype=jnp.int32)[None, :, None]
    buffer = jnp.zeros((STREAMS, N_SEQ, EXPERTS, CAP, D), jnp.bfloat16)
    buffer = buffer.at[stream_idx, device_idx, grouped, slots].set(rows)
    by_expert = jnp.moveaxis(buffer, 2, 0)
    slice_width = FF // N_EXP

    def run_expert(args):
        tokens_e, gate_e, up_e, down_e = args
        flat = tokens_e.reshape(-1, D)
        total = jnp.zeros((flat.shape[0], D), jnp.float32)
        for piece in range(N_EXP):
            low = piece * slice_width
            high = low + slice_width
            gate_p = jnp.dot(flat, gate_e[:, low:high], preferred_element_type=jnp.float32)
            up_p = jnp.dot(flat, up_e[:, low:high], preferred_element_type=jnp.float32)
            active = (jax.nn.silu(gate_p) * up_p).astype(jnp.bfloat16)
            part = jnp.dot(active, down_e[low:high], preferred_element_type=jnp.float32).astype(jnp.bfloat16)
            total = total + lax.optimization_barrier(part).astype(jnp.float32)
        return total.astype(jnp.bfloat16).reshape(tokens_e.shape)
    expert_out = lax.map(run_expert, (by_expert, w_gate, w_up, w_down))
    picked = expert_out[grouped, stream_idx, device_idx, slots]
    picked = picked.reshape(STREAMS, LEN, 2, D).astype(jnp.float32)
    moe = lax.optimization_barrier(jnp.sum(picked * gates[..., None], axis=2))
    mixed = (hidden_one + moe).astype(jnp.bfloat16)
    return (attended, mixed)
```

```python
import jax
import jax.numpy as jnp
from jax import lax
from jax.experimental import pallas as pl
from jax.experimental.pallas import tpu as pltpu
from jax.sharding import Mesh
from jax.sharding import PartitionSpec as P

HEAD = 128
CAP = 2
BLOCK = 128
TOK = 32
D = 2048
F32 = jnp.float32
BF16 = jnp.bfloat16
VMEM_LIMIT = 48 * 1024 * 1024


def vmem_call(body, out_shape, n_in, smem=()):
    return pl.pallas_call(
        body,
        out_shape=out_shape,
        in_specs=[
            pl.BlockSpec(memory_space=pltpu.SMEM if i in smem else pltpu.VMEM) for i in range(n_in)
        ],
        out_specs=jax.tree.map(lambda _: pl.BlockSpec(memory_space=pltpu.VMEM), out_shape),
        compiler_params=pltpu.CompilerParams(vmem_limit_bytes=VMEM_LIMIT),
    )


def attend_kernel(place_ref, mask_ref, query_ref, kv_ref, out_ref):
    x, c = place_ref[0], place_ref[1]
    n_key = kv_ref.shape[0] * TOK
    keys = kv_ref[:, :TOK].reshape(n_key, HEAD)
    values = kv_ref[:, TOK:].reshape(n_key, HEAD)
    key_row = lax.broadcasted_iota(jnp.int32, (1, n_key), 1)
    key_x, key_c, key_z, key_t = key_row // 512, key_row // 256 % 2, key_row // 32 % 8, key_row % 32
    key_pos = key_x * 512 + key_z * 64 + key_c * 32 + key_t
    block_row = lax.broadcasted_iota(jnp.int32, (16, n_key), 0)
    key_onehot = (block_row == jnp.broadcast_to(key_pos // BLOCK, (16, n_key))).astype(BF16)
    row_i = lax.broadcasted_iota(jnp.int32, (16, 16), 0)
    col_i = lax.broadcasted_iota(jnp.int32, (16, 16), 1)
    live = ((mask_ref[...] > 0) | (row_i == col_i)).astype(BF16)
    seen = jnp.dot(live, key_onehot, preferred_element_type=F32)
    seen_row = lax.broadcasted_iota(jnp.int32, (16, n_key), 0)
    scale = HEAD ** (-0.5)
    for j in range(4):
        mine = jnp.sum(jnp.where(seen_row == x * 4 + j, seen, 0.0), axis=0, keepdims=True)
        rows = query_ref[2 * j : 2 * j + 2, :TOK].reshape(2 * TOK, HEAD)
        row = lax.broadcasted_iota(jnp.int32, (2 * TOK, 1), 0)
        query_pos = x * 512 + (2 * j + row // 32) * 64 + c * 32 + row % 32
        allowed = (jnp.broadcast_to(mine, (2 * TOK, n_key)) > 0.5) & (key_pos <= query_pos)
        scores = lax.dot_general(rows, keys, (((1,), (1,)), ((), ())), preferred_element_type=F32)
        scores = jnp.where(allowed, scores * scale, -1e30)
        top = jnp.max(scores, axis=-1, keepdims=True)
        weights = jnp.exp(scores - top)
        total = jnp.sum(weights, axis=-1, keepdims=True)
        update = jnp.dot(weights.astype(BF16), values, preferred_element_type=F32)
        out_ref[2 * j : 2 * j + 2] = (update / total).astype(BF16).reshape(2, TOK, HEAD)


def project_kernel(
    att_ref, weight_ref, residual_ref, gain_ref, router_ref, ids_ref, spread_ref,
    attended_ref, hidden_ref, gates_ref, buffer_ref,
):
    attended = jnp.concatenate([att_ref[h] for h in range(8)], axis=1)
    attended_ref[...] = attended
    low, high = attended[:, :512], attended[:, 512:]
    pieces = []
    for y in range(8):
        piece = jnp.dot(low, weight_ref[y], preferred_element_type=F32) + jnp.dot(
            high, weight_ref[8 + y], preferred_element_type=F32
        )
        pieces.append(piece.astype(BF16).astype(F32))
    hidden = residual_ref[...].astype(F32) + jnp.concatenate(pieces, axis=1)
    hidden_ref[...] = hidden
    meansq = jnp.mean(hidden * hidden, axis=-1, keepdims=True)
    normed = (hidden * lax.rsqrt(meansq + 1e-06) * gain_ref[...]).astype(BF16)
    logits = jnp.dot(normed, router_ref[...], preferred_element_type=F32)
    expert = lax.broadcasted_iota(jnp.int32, logits.shape, 1)
    first = jnp.sum(jnp.where(expert == ids_ref[:, 0:1], logits, 0.0), axis=-1, keepdims=True)
    second = jnp.sum(jnp.where(expert == ids_ref[:, 1:2], logits, 0.0), axis=-1, keepdims=True)
    gate = jax.nn.sigmoid(first - second)
    gates_ref[...] = jnp.concatenate([gate, 1.0 - gate], axis=1)
    buffer_ref[...] = jnp.dot(spread_ref[...], normed, preferred_element_type=F32).astype(BF16)


def expert_kernel(rows_ref, gate_ref, up_ref, down_ref, out_ref):
    rows = rows_ref[...]
    gate = jnp.dot(rows, gate_ref[...], preferred_element_type=F32)
    up = jnp.dot(rows, up_ref[...], preferred_element_type=F32)
    active = (gate / (1.0 + jnp.exp(-gate)) * up).astype(BF16)
    out_ref[...] = jnp.dot(active, down_ref[...], preferred_element_type=F32).astype(BF16)


def expert_call(rows, gate, up, down):
    step = 256
    whole = lambda a: pl.BlockSpec(a.shape, lambda i: (0, 0))
    return pl.pallas_call(
        expert_kernel,
        grid=(rows.shape[0] // step,),
        in_specs=[pl.BlockSpec((step, D), lambda i: (i, 0)), whole(gate), whole(up), whole(down)],
        out_specs=pl.BlockSpec((step, D), lambda i: (i, 0)),
        out_shape=jax.ShapeDtypeStruct(rows.shape, BF16),
        compiler_params=pltpu.CompilerParams(vmem_limit_bytes=VMEM_LIMIT),
    )(rows, gate, up, down)


def combine_kernel(hidden_ref, gates_ref, first_ref, second_ref, rows_ref, out_ref):
    rows = rows_ref[...]
    first = jnp.dot(first_ref[...], rows, preferred_element_type=F32)
    second = jnp.dot(second_ref[...], rows, preferred_element_type=F32)
    moe = first * gates_ref[:, 0:1] + second * gates_ref[:, 1:2]
    out_ref[...] = (hidden_ref[...] + moe).astype(BF16)


def shards(
    residual,
    queries,
    keys,
    values,
    block_mask,
    out_weight,
    norm_gain,
    router,
    route_ids,
    w_gate,
    w_up,
    w_down,
):
    x, c = lax.axis_index("x"), lax.axis_index("c")
    place = jnp.stack([x, c]).astype(jnp.int32)
    half = lax.dynamic_slice_in_dim(out_weight, c * 512, 512, axis=0)
    weight = lax.all_gather(half, ("c", "y"), axis=0)

    by_head = jnp.stack(
        [a[0].reshape(TOK, 8, HEAD).transpose(1, 0, 2) for a in (queries, keys, values)], axis=1
    ).reshape(8, 3 * TOK, HEAD)
    by_token = lax.all_to_all(by_head, "z", split_axis=0, concat_axis=0, tiled=True)
    kv = jnp.broadcast_to(by_token[None, :, TOK:], (8, 8, 2 * TOK, HEAD))
    kv = lax.all_to_all(kv, ("x", "c"), split_axis=0, concat_axis=0, tiled=True)
    att = vmem_call(attend_kernel, jax.ShapeDtypeStruct((8, TOK, HEAD), BF16), 4, smem=(0,))(
        place, block_mask[0], by_token, kv.reshape(64, 2 * TOK, HEAD)
    )
    att = lax.all_to_all(att, "z", split_axis=0, concat_axis=0, tiled=True)

    ids = route_ids[0]
    expert_count = router.shape[1]
    slot_count = expert_count * CAP
    assigned = ids.reshape(2 * TOK)
    onehot = (assigned[:, None] == jnp.arange(expert_count, dtype=jnp.int32)).astype(F32)
    order = jnp.arange(2 * TOK, dtype=jnp.int32)
    lower = (order[:, None] > order[None, :]).astype(F32)
    earlier = jnp.dot(lower, onehot)
    slots = jnp.sum(earlier * onehot, axis=-1).astype(jnp.int32).reshape(TOK, 2)
    spot = ids * CAP + slots
    spots = jnp.arange(slot_count, dtype=jnp.int32)
    first = (spot[:, 0:1] == spots).astype(BF16)
    second = (spot[:, 1:2] == spots).astype(BF16)
    spread = (first + second).T

    attended, hidden, gates, buffer = vmem_call(
        project_kernel,
        (
            jax.ShapeDtypeStruct((TOK, 8 * HEAD), BF16),
            jax.ShapeDtypeStruct((TOK, D), F32),
            jax.ShapeDtypeStruct((TOK, 2), F32),
            jax.ShapeDtypeStruct((slot_count, D), BF16),
        ),
        7,
    )(att, weight, residual[0], norm_gain[None], router, ids, spread)

    seq = ("x", "z", "c")
    arrived = lax.all_to_all(
        buffer.reshape(expert_count, CAP, D), seq, split_axis=0, concat_axis=0, tiled=True
    )
    rows = lax.all_gather(arrived.reshape(slot_count, D), "y", axis=0, tiled=True)
    parts = expert_call(rows, w_gate[0], w_up[0], w_down[0])
    summed = lax.psum_scatter(parts, "y", scatter_dimension=0, tiled=True)
    returned = lax.all_to_all(
        summed.reshape(expert_count, CAP, D), seq, split_axis=0, concat_axis=0, tiled=True
    )
    mixed = vmem_call(combine_kernel, jax.ShapeDtypeStruct((TOK, D), BF16), 5)(
        hidden, gates, first, second, returned.reshape(slot_count, D)
    )
    return (attended[None], mixed[None])


def solution(mesh):
    mesh = Mesh(mesh.devices.reshape(4, 8, 2, 8), ("x", "z", "c", "y"))
    seq = ("x", "z", "c")
    placed = (
        P("y", seq, None),
        P("y", seq, None),
        P("y", seq, None),
        P("y", seq, None),
        P("y", None, None),
        P(None, "y"),
        P(),
        P(),
        P("y", seq, None),
        P(seq, None, "y"),
        P(seq, None, "y"),
        P(seq, "y", None),
    )
    return jax.shard_map(
        shards,
        mesh=mesh,
        in_specs=placed,
        out_specs=(P("y", seq, None), P("y", seq, None)),
        check_vma=False,
    )
```

```python
import jax
import jax.numpy as jnp
from jax import lax
from jax.experimental import pallas as pl
from jax.experimental.pallas import tpu as pltpu
from jax.sharding import Mesh
from jax.sharding import PartitionSpec as P

HEAD = 128
CAP = 2
BLOCK = 128
TOK = 32
D = 2048
CHUNK = 256
EXPERTS = 64
F32 = jnp.float32
BF16 = jnp.bfloat16
VMEM_LIMIT = 48 * 1024 * 1024


def vmem_call(body, out_shape, n_in, smem=()):
    return pl.pallas_call(
        body,
        out_shape=out_shape,
        in_specs=[
            pl.BlockSpec(memory_space=pltpu.SMEM if i in smem else pltpu.VMEM) for i in range(n_in)
        ],
        out_specs=jax.tree.map(lambda _: pl.BlockSpec(memory_space=pltpu.VMEM), out_shape),
        compiler_params=pltpu.CompilerParams(vmem_limit_bytes=VMEM_LIMIT),
    )


def slot_spots(ids):
    expert = lax.broadcasted_iota(jnp.int32, (TOK, EXPERTS), 1)
    first = jnp.where(expert == ids[:, 0:1], 1.0, 0.0)
    second = jnp.where(expert == ids[:, 1:2], 1.0, 0.0)
    row = lax.broadcasted_iota(jnp.int32, (TOK, TOK), 0)
    col = lax.broadcasted_iota(jnp.int32, (TOK, TOK), 1)
    lower = jnp.where(row > col, 1.0, 0.0).astype(BF16)
    earlier = jnp.dot(lower, (first + second).astype(BF16), preferred_element_type=F32)
    base = CAP * expert.astype(F32) + earlier
    spot_first = jnp.sum(first * base, axis=-1, keepdims=True)
    spot_second = jnp.sum(second * base, axis=-1, keepdims=True)
    return first, second, spot_first, spot_second


def pack_kernel(place_ref, query_ref, key_ref, value_ref, residual_ref, ids_ref, out_ref):
    z = place_ref[1]
    _, _, spot_first, spot_second = slot_spots(ids_ref[...])
    lane = lax.broadcasted_iota(jnp.int32, (TOK, 8 * TOK), 1)
    token = lax.broadcasted_iota(jnp.int32, (TOK, 8 * TOK), 0)
    here = lane == z * TOK + token
    spread_first = jnp.sum(jnp.where(here, spot_first, 0.0), axis=0, keepdims=True)
    spread_second = jnp.sum(jnp.where(here, spot_second, 0.0), axis=0, keepdims=True)
    row = lax.broadcasted_iota(jnp.int32, (16, HEAD), 0)
    tile = jnp.where(row == 0, spread_first[:, :HEAD], 0.0)
    tile = jnp.where(row == 1, spread_first[:, HEAD:], tile)
    tile = jnp.where(row == 2, spread_second[:, :HEAD], tile)
    tile = jnp.where(row == 3, spread_second[:, HEAD:], tile).astype(BF16)
    for h in range(8):
        cols = slice(h * HEAD, (h + 1) * HEAD)
        out_ref[h, 0:32] = query_ref[:, cols]
        out_ref[h, 32:64] = key_ref[:, cols]
        out_ref[h, 64:96] = value_ref[:, cols]
        out_ref[h, 96:128] = residual_ref[:, h * CHUNK : h * CHUNK + HEAD]
        out_ref[h, 128:160] = residual_ref[:, h * CHUNK + HEAD : (h + 1) * CHUNK]
        out_ref[h, 160:176] = tile


def attend_kernel(place_ref, mask_ref, packed_ref, kv_ref, out_ref):
    x, c = place_ref[0], place_ref[2]
    n_key = kv_ref.shape[0] * TOK
    keys = kv_ref[:, :TOK].reshape(n_key, HEAD)
    values = kv_ref[:, TOK:].reshape(n_key, HEAD)
    key_row = lax.broadcasted_iota(jnp.int32, (1, n_key), 1)
    key_x, key_c, key_z, key_t = key_row // 512, key_row // 256 % 2, key_row // 32 % 8, key_row % 32
    key_pos = key_x * 512 + key_z * 64 + key_c * 32 + key_t
    block_row = lax.broadcasted_iota(jnp.int32, (16, n_key), 0)
    key_onehot = (block_row == jnp.broadcast_to(key_pos // BLOCK, (16, n_key))).astype(BF16)
    row_i = lax.broadcasted_iota(jnp.int32, (16, 16), 0)
    col_i = lax.broadcasted_iota(jnp.int32, (16, 16), 1)
    live = ((mask_ref[...] > 0) | (row_i == col_i)).astype(BF16)
    seen = jnp.dot(live, key_onehot, preferred_element_type=F32)
    seen_row = lax.broadcasted_iota(jnp.int32, (16, n_key), 0)
    scale = HEAD ** (-0.5)
    for j in range(4):
        mine = jnp.sum(jnp.where(seen_row == x * 4 + j, seen, 0.0), axis=0, keepdims=True)
        rows = packed_ref[2 * j : 2 * j + 2, :TOK].reshape(2 * TOK, HEAD)
        row = lax.broadcasted_iota(jnp.int32, (2 * TOK, 1), 0)
        query_pos = x * 512 + (2 * j + row // 32) * 64 + c * 32 + row % 32
        allowed = (jnp.broadcast_to(mine, (2 * TOK, n_key)) > 0.5) & (key_pos <= query_pos)
        scores = lax.dot_general(rows, keys, (((1,), (1,)), ((), ())), preferred_element_type=F32)
        scores = jnp.where(allowed, scores * scale, -1e30)
        top = jnp.max(scores, axis=-1, keepdims=True)
        weights = jnp.exp(scores - top)
        total = jnp.sum(weights, axis=-1, keepdims=True)
        update = jnp.dot(weights.astype(BF16), values, preferred_element_type=F32)
        attended = (update / total).astype(BF16)
        for z in range(8):
            out_ref[z, 2 * j * TOK : 2 * (j + 1) * TOK] = attended


def project_kernel(
    place_ref, att_ref, weight_ref, packed_ref, gain_ref, attended_ref, projected_ref, buffer_ref
):
    z = place_ref[1]
    mine = pl.ds(pl.multiple_of(z * TOK, TOK), TOK)
    attended_ref[...] = jnp.concatenate([att_ref[h, mine] for h in range(8)], axis=1)
    attended = jnp.concatenate([att_ref[h] for h in range(8)], axis=1)
    projected = jnp.dot(attended, weight_ref[...], preferred_element_type=F32).astype(BF16)
    projected_ref[...] = projected.reshape(8, TOK, CHUNK)
    residual = jnp.concatenate(
        [packed_ref[:, 96:128].reshape(8 * TOK, HEAD), packed_ref[:, 128:160].reshape(8 * TOK, HEAD)],
        axis=1,
    )
    hidden = residual.astype(F32) + projected.astype(F32)
    scaled = (hidden * gain_ref[pl.ds(z, 1), :]).astype(BF16)
    spots = jnp.sum(packed_ref[:, 160:176].astype(F32), axis=0)
    spot_first = jnp.concatenate([spots[0:1], spots[1:2]], axis=1)
    spot_second = jnp.concatenate([spots[2:3], spots[3:4]], axis=1)
    row = lax.broadcasted_iota(jnp.int32, (8 * EXPERTS * CAP, 1), 0)
    row_spot = (row // 16 * CAP + row % CAP).astype(F32)
    row_block = row // CAP % 8
    col_block = lax.broadcasted_iota(jnp.int32, (1, 8 * TOK), 1) // TOK
    taken = (spot_first == row_spot) | (spot_second == row_spot)
    spread = jnp.where(taken & (row_block == col_block), 1.0, 0.0).astype(BF16)
    rows = jnp.dot(spread, scaled, preferred_element_type=F32).astype(BF16)
    buffer_ref[...] = rows.reshape(EXPERTS, 16, CHUNK)


def gates_kernel(
    projected_ref, residual_ref, gain_ref, router_ref, ids_ref,
    hidden_ref, gates_ref, first_ref, second_ref,
):
    projected = jnp.concatenate([projected_ref[z] for z in range(8)], axis=1)
    hidden = residual_ref[...].astype(F32) + projected.astype(F32)
    hidden_ref[...] = hidden
    meansq = jnp.mean(hidden * hidden, axis=-1, keepdims=True)
    normed = (hidden * lax.rsqrt(meansq + 1e-06) * gain_ref[...]).astype(BF16)
    logits = jnp.dot(normed, router_ref[...], preferred_element_type=F32)
    first, second, spot_first, spot_second = slot_spots(ids_ref[...])
    logit_first = jnp.sum(first * logits, axis=-1, keepdims=True)
    logit_second = jnp.sum(second * logits, axis=-1, keepdims=True)
    gate = jax.nn.sigmoid(logit_first - logit_second)
    gates_ref[...] = jnp.concatenate([gate, 1.0 - gate], axis=1)
    spot = lax.broadcasted_iota(jnp.int32, (TOK, EXPERTS * CAP), 1).astype(F32)
    first_ref[...] = jnp.where(spot == spot_first, 1.0, 0.0).astype(BF16)
    second_ref[...] = jnp.where(spot == spot_second, 1.0, 0.0).astype(BF16)


def expert_kernel(rows_ref, inverse_ref, gate_ref, up_ref, out_ref):
    count = rows_ref.shape[0] * 128
    gate = up = squares = None
    for z in range(8):
        piece = rows_ref[:, :, z].reshape(count, CHUNK)
        span = slice(z * CHUNK, (z + 1) * CHUNK)
        plain = piece.astype(F32) * inverse_ref[z : z + 1, :]
        gate_z = jnp.dot(piece, gate_ref[span], preferred_element_type=F32)
        up_z = jnp.dot(piece, up_ref[span], preferred_element_type=F32)
        squares_z = plain * plain
        if z == 0:
            gate, up, squares = gate_z, up_z, squares_z
        else:
            gate, up, squares = gate + gate_z, up + up_z, squares + squares_z
    meansq = jnp.sum(squares, axis=-1, keepdims=True) * (1.0 / D)
    factor = lax.rsqrt(meansq + 1e-06)
    gate, up = gate * factor, up * factor
    active = (gate / (1.0 + jnp.exp(-gate)) * up).astype(BF16)
    width = active.shape[1]
    row = lax.broadcasted_iota(jnp.int32, (width, width), 0)
    col = lax.broadcasted_iota(jnp.int32, (width, width), 1)
    same = jnp.where(row == col, 1.0, 0.0).astype(BF16)
    for s in range(rows_ref.shape[0]):
        out_ref[s] = lax.dot_general(
            same,
            active[s * 128 : (s + 1) * 128],
            (((1,), (1,)), ((), ())),
            preferred_element_type=F32,
        ).astype(BF16)


def expert_call(rows, inverse, gate, up):
    step = 2
    width = gate.shape[1]
    whole = lambda a: pl.BlockSpec(a.shape, lambda i: (0, 0))
    return pl.pallas_call(
        expert_kernel,
        grid=(8 // step,),
        in_specs=[
            pl.BlockSpec((step, 4, 8, 2, 16, CHUNK), lambda i: (i, 0, 0, 0, 0, 0)),
            whole(inverse),
            whole(gate),
            whole(up),
        ],
        out_specs=pl.BlockSpec((step, width, 128), lambda i: (i, 0, 0)),
        out_shape=jax.ShapeDtypeStruct((8, width, 128), BF16),
        compiler_params=pltpu.CompilerParams(vmem_limit_bytes=VMEM_LIMIT),
    )(rows, inverse, gate, up)


def down_kernel(active_ref, down_ref, out_ref):
    row = lax.broadcasted_iota(jnp.int32, (128, 128), 0)
    col = lax.broadcasted_iota(jnp.int32, (128, 128), 1)
    source = row // 32 * 32 + row // 2 % 2 * 16 + row // 4 % 8 * 2 + row % 2
    order = jnp.where(col == source, 1.0, 0.0).astype(BF16)
    total = None
    for y in range(8):
        active = lax.dot_general(
            order, active_ref[y], (((1,), (1,)), ((), ())), preferred_element_type=F32
        ).astype(BF16)
        part = jnp.dot(active, down_ref[y], preferred_element_type=F32)
        total = part if y == 0 else total + part
    out_ref[...] = total.astype(BF16)


def down_call(active, down):
    step = 512
    return pl.pallas_call(
        down_kernel,
        grid=(D // step,),
        in_specs=[
            pl.BlockSpec(active.shape, lambda i: (0, 0, 0)),
            pl.BlockSpec((8, down.shape[1], step), lambda i: (0, 0, i)),
        ],
        out_specs=pl.BlockSpec((128, step), lambda i: (0, i)),
        out_shape=jax.ShapeDtypeStruct((128, D), BF16),
        compiler_params=pltpu.CompilerParams(vmem_limit_bytes=VMEM_LIMIT),
    )(active, down)


def combine_kernel(hidden_ref, gates_ref, first_ref, second_ref, rows_ref, out_ref):
    rows = rows_ref[...]
    first = jnp.dot(first_ref[...], rows, preferred_element_type=F32)
    second = jnp.dot(second_ref[...], rows, preferred_element_type=F32)
    moe = first * gates_ref[:, 0:1] + second * gates_ref[:, 1:2]
    out_ref[...] = (hidden_ref[...] + moe).astype(BF16)


def shards(
    residual,
    queries,
    keys,
    values,
    block_mask,
    out_weight,
    norm_gain,
    router,
    route_ids,
    w_gate,
    w_up,
    w_down,
):
    seq = ("x", "z", "c")
    place = jnp.stack([lax.axis_index(a) for a in seq]).astype(jnp.int32)
    ids = route_ids[0]
    shape = lambda *s: jax.ShapeDtypeStruct(s, BF16)
    swap = lambda a, axes: lax.all_to_all(a, axes, split_axis=0, concat_axis=0, tiled=True)

    down = lax.all_gather(w_down[0], "y", axis=0)
    weight = lax.ppermute(
        out_weight, ("z", "y"), [(z * 8 + y, y * 8 + z) for z in range(8) for y in range(8)]
    )

    packed = vmem_call(pack_kernel, shape(8, 176, HEAD), 6, smem=(0,))(
        place, queries[0], keys[0], values[0], residual[0], ids
    )
    packed = swap(packed, "z")
    kv = jnp.broadcast_to(packed[None, :, 32:96], (8, 8, 2 * TOK, HEAD))
    kv = swap(kv, ("x", "c"))
    att = vmem_call(attend_kernel, shape(8, 8 * TOK, HEAD), 4, smem=(0,))(
        place, block_mask[0], packed, kv.reshape(64, 2 * TOK, HEAD)
    )
    att = swap(att, "z")
    attended, projected, buffer = vmem_call(
        project_kernel,
        (shape(TOK, 8 * HEAD), shape(8, TOK, CHUNK), shape(EXPERTS, 16, CHUNK)),
        5,
        smem=(0,),
    )(place, att, weight, packed, norm_gain.reshape(8, CHUNK))

    rows = lax.all_gather(swap(buffer, seq), "y", axis=0)
    projected = swap(projected, "z")
    hidden, gates, first, second = vmem_call(
        gates_kernel,
        (
            jax.ShapeDtypeStruct((TOK, D), F32),
            jax.ShapeDtypeStruct((TOK, 2), F32),
            shape(TOK, EXPERTS * CAP),
            shape(TOK, EXPERTS * CAP),
        ),
        5,
    )(projected, residual[0], norm_gain[None], router, ids)

    active = expert_call(
        rows.reshape(8, 4, 8, 2, 16, CHUNK), (1.0 / norm_gain).reshape(8, CHUNK), w_gate[0], w_up[0]
    )
    out = down_call(swap(active, "y"), down)
    returned = swap(out.reshape(EXPERTS, CAP, D), seq)
    mixed = vmem_call(combine_kernel, shape(TOK, D), 5)(
        hidden, gates, first, second, returned.reshape(EXPERTS * CAP, D)
    )
    return (attended[None], mixed[None])


def solution(mesh):
    mesh = Mesh(mesh.devices.reshape(4, 8, 2, 8), ("x", "z", "c", "y"))
    seq = ("x", "z", "c")
    placed = (
        P("y", seq, None),
        P("y", seq, None),
        P("y", seq, None),
        P("y", seq, None),
        P("y", None, None),
        P(None, "y"),
        P(),
        P(),
        P("y", seq, None),
        P(seq, None, "y"),
        P(seq, None, "y"),
        P(seq, "y", None),
    )
    return jax.shard_map(
        shards,
        mesh=mesh,
        in_specs=placed,
        out_specs=(P("y", seq, None), P("y", seq, None)),
        check_vma=False,
    )
```

```python
import jax
import jax.numpy as jnp
from jax import lax
from jax.experimental import pallas as pl
from jax.experimental.pallas import tpu as pltpu
from jax.sharding import Mesh
from jax.sharding import PartitionSpec as P

HEAD = 128
CAP = 2
BLOCK = 128
TOK = 32
D = 2048
CHUNK = 256
EXPERTS = 64
F32 = jnp.float32
BF16 = jnp.bfloat16
VMEM_LIMIT = 48 * 1024 * 1024


def vmem_call(body, out_shape, n_in, smem=(), hbm=(), scratch=(), limit=VMEM_LIMIT):
    space = lambda i: pltpu.SMEM if i in smem else pl.ANY if i in hbm else pltpu.VMEM
    return pl.pallas_call(
        body,
        out_shape=out_shape,
        in_specs=[pl.BlockSpec(memory_space=space(i)) for i in range(n_in)],
        out_specs=jax.tree.map(lambda _: pl.BlockSpec(memory_space=pltpu.VMEM), out_shape),
        scratch_shapes=list(scratch),
        compiler_params=pltpu.CompilerParams(vmem_limit_bytes=limit),
    )


def slot_spots(ids):
    expert = lax.broadcasted_iota(jnp.int32, (TOK, EXPERTS), 1)
    first = jnp.where(expert == ids[:, 0:1], 1.0, 0.0)
    second = jnp.where(expert == ids[:, 1:2], 1.0, 0.0)
    row = lax.broadcasted_iota(jnp.int32, (TOK, TOK), 0)
    col = lax.broadcasted_iota(jnp.int32, (TOK, TOK), 1)
    lower = jnp.where(row > col, 1.0, 0.0).astype(BF16)
    earlier = jnp.dot(lower, (first + second).astype(BF16), preferred_element_type=F32)
    base = CAP * expert.astype(F32) + earlier
    spot_first = jnp.sum(first * base, axis=-1, keepdims=True)
    spot_second = jnp.sum(second * base, axis=-1, keepdims=True)
    return first, second, spot_first, spot_second


def chunk_of(z, y):
    return lax.rem(z - y + 8, 8)


def holder_of(chunk, y):
    return lax.rem(chunk + y, 8)


def pack_kernel(
    place_ref, query_hbm, key_hbm, value_hbm, residual_hbm, ids_hbm, out_ref,
    query_ref, key_ref, value_ref, residual_ref, ids_ref, sems,
):
    pairs = (
        (ids_hbm, ids_ref), (query_hbm, query_ref), (key_hbm, key_ref), (value_hbm, value_ref),
        (residual_hbm, residual_ref),
    )
    copies = [pltpu.make_async_copy(a, b, sems.at[i]) for i, (a, b) in enumerate(pairs)]
    for copy in copies:
        copy.start()
    z, y = place_ref[1], place_ref[3]
    copies[0].wait()
    expert = lax.broadcasted_iota(jnp.int32, (EXPERTS, TOK), 0)
    first = jnp.where(expert == ids_ref[0:1], 1.0, 0.0)
    second = jnp.where(expert == ids_ref[1:2], 1.0, 0.0)
    row = lax.broadcasted_iota(jnp.int32, (TOK, TOK), 0)
    col = lax.broadcasted_iota(jnp.int32, (TOK, TOK), 1)
    upper = jnp.where(row < col, 1.0, 0.0).astype(BF16)
    earlier = jnp.dot((first + second).astype(BF16), upper, preferred_element_type=F32)
    base = CAP * expert.astype(F32) + earlier
    spot_first = jnp.sum(first * base, axis=0, keepdims=True)
    spot_second = jnp.sum(second * base, axis=0, keepdims=True)
    row = lax.broadcasted_iota(jnp.int32, (16, TOK), 0)
    tile = jnp.where(row < 2, spot_first, jnp.where(row < 4, spot_second, 0.0)).astype(BF16)
    lane = lax.broadcasted_iota(jnp.int32, (TOK, 2 * HEAD), 1)
    token = lax.broadcasted_iota(jnp.int32, (TOK, 2 * HEAD), 0)
    here = jnp.where(lane == z * TOK + token, 1.0, 0.0).astype(BF16)
    tile = jnp.dot(tile, here, preferred_element_type=F32)
    row = lax.broadcasted_iota(jnp.int32, (16, HEAD), 0)
    tile = jnp.where(row % 2 == 0, tile[:, :HEAD], tile[:, HEAD:]).astype(BF16)
    for copy in copies[1:]:
        copy.wait()
    for h in range(8):
        cols = slice(h * HEAD, (h + 1) * HEAD)
        out_ref[h, 0:32] = query_ref[:, cols]
        out_ref[h, 32:64] = key_ref[:, cols]
        out_ref[h, 64:96] = value_ref[:, cols]
        out_ref[h, 160:176] = tile
        holder = holder_of(h, y)
        out_ref[holder, 96:128] = residual_ref[:, h * CHUNK : h * CHUNK + HEAD]
        out_ref[holder, 128:160] = residual_ref[:, h * CHUNK + HEAD : (h + 1) * CHUNK]


def spread_kernel(packed_ref, out_ref):
    for i in range(8):
        out_ref[i] = packed_ref[:, 32:96]


def attend_kernel(place_ref, mask_ref, packed_ref, kv_ref, _, out_ref):
    x, c = place_ref[0], place_ref[2]
    n_key = kv_ref.shape[0] * TOK
    keys = kv_ref[:, :TOK].reshape(n_key, HEAD)
    values = kv_ref[:, TOK:].reshape(n_key, HEAD)
    key_row = lax.broadcasted_iota(jnp.int32, (1, n_key), 1)
    key_x, key_c, key_z, key_t = key_row // 512, key_row // 256 % 2, key_row // 32 % 8, key_row % 32
    key_pos = key_x * 512 + key_z * 64 + key_c * 32 + key_t
    block_row = lax.broadcasted_iota(jnp.int32, (16, n_key), 0)
    key_onehot = (block_row == jnp.broadcast_to(key_pos // BLOCK, (16, n_key))).astype(BF16)
    row_i = lax.broadcasted_iota(jnp.int32, (16, 16), 0)
    col_i = lax.broadcasted_iota(jnp.int32, (16, 16), 1)
    live = ((mask_ref[...] > 0) | (row_i == col_i)).astype(BF16)
    seen = jnp.dot(live, key_onehot, preferred_element_type=F32)
    seen_row = lax.broadcasted_iota(jnp.int32, (16, n_key), 0)
    scale = HEAD ** (-0.5)
    for j in range(4):
        mine = jnp.sum(jnp.where(seen_row == x * 4 + j, seen, 0.0), axis=0, keepdims=True)
        rows = packed_ref[2 * j : 2 * j + 2, :TOK].reshape(2 * TOK, HEAD)
        row = lax.broadcasted_iota(jnp.int32, (2 * TOK, 1), 0)
        query_pos = x * 512 + (2 * j + row // 32) * 64 + c * 32 + row % 32
        allowed = (jnp.broadcast_to(mine, (2 * TOK, n_key)) > 0.5) & (key_pos <= query_pos)
        scores = lax.dot_general(rows, keys, (((1,), (1,)), ((), ())), preferred_element_type=F32)
        scores = jnp.where(allowed, scores * scale, -1e30)
        top = jnp.max(scores, axis=-1, keepdims=True)
        weights = jnp.exp(scores - top)
        total = jnp.sum(weights, axis=-1, keepdims=True)
        update = jnp.dot(weights.astype(BF16), values, preferred_element_type=F32)
        attended = (update / total).astype(BF16)
        for z in range(8):
            out_ref[z, 2 * j * TOK : 2 * (j + 1) * TOK] = attended


def project_kernel(
    place_ref, att_ref, own_ref, core_ref, x_ref, x_core_ref, packed_ref, gain_ref, attended_ref, projected_ref, buffer_ref
):
    z, y = place_ref[1], place_ref[3]
    mine = pl.ds(pl.multiple_of(z * TOK, TOK), TOK)
    attended_ref[...] = jnp.concatenate([att_ref[h, mine] for h in range(8)], axis=1)
    quarter = place_ref[0] % 2 * 2 + place_ref[2]
    total = None
    for ref, flip in ((own_ref, 0), (core_ref, 1), (x_ref, 2), (x_core_ref, 3)):
        rows = quarter ^ flip
        attended = jnp.concatenate([att_ref[2 * rows], att_ref[2 * rows + 1]], axis=1)
        part = jnp.dot(attended, ref[...], preferred_element_type=F32)
        total = part if total is None else total + part
    projected = total.astype(BF16)
    projected_ref[...] = projected.reshape(8, TOK, CHUNK)
    residual = jnp.concatenate(
        [packed_ref[:, 96:128].reshape(8 * TOK, HEAD), packed_ref[:, 128:160].reshape(8 * TOK, HEAD)],
        axis=1,
    )
    hidden = residual.astype(F32) + projected.astype(F32)
    scaled = (hidden * gain_ref[pl.ds(chunk_of(z, y), 1), :]).astype(BF16)
    spots = jnp.sum(packed_ref[:, 160:176].astype(F32), axis=0)
    spot_first = jnp.concatenate([spots[0:1], spots[1:2]], axis=1)
    spot_second = jnp.concatenate([spots[2:3], spots[3:4]], axis=1)
    row = lax.broadcasted_iota(jnp.int32, (8 * EXPERTS * CAP, 1), 0)
    row_spot = (row // 16 * CAP + row % CAP).astype(F32)
    row_block = row // CAP % 8
    col_block = lax.broadcasted_iota(jnp.int32, (1, 8 * TOK), 1) // TOK
    taken = (spot_first == row_spot) | (spot_second == row_spot)
    spread = jnp.where(taken & (row_block == col_block), 1.0, 0.0).astype(BF16)
    rows = jnp.dot(spread, scaled, preferred_element_type=F32).astype(BF16)
    buffer_ref[...] = rows.reshape(EXPERTS, 16, CHUNK)


def gates_kernel(
    place_ref, projected_ref, residual_ref, gain_ref, router_ref, ids_ref,
    hidden_ref, gates_ref, first_ref, second_ref,
):
    y = place_ref[3]
    projected = jnp.concatenate([projected_ref[holder_of(k, y)] for k in range(8)], axis=1)
    hidden = residual_ref[...].astype(F32) + projected.astype(F32)
    hidden_ref[...] = hidden
    meansq = jnp.mean(hidden * hidden, axis=-1, keepdims=True)
    normed = (hidden * lax.rsqrt(meansq + 1e-06) * gain_ref[...]).astype(BF16)
    logits = jnp.dot(normed, router_ref[...], preferred_element_type=F32)
    first, second, spot_first, spot_second = slot_spots(ids_ref[...])
    logit_first = jnp.sum(first * logits, axis=-1, keepdims=True)
    logit_second = jnp.sum(second * logits, axis=-1, keepdims=True)
    gate = jax.nn.sigmoid(logit_first - logit_second)
    gates_ref[...] = jnp.concatenate([gate, 1.0 - gate], axis=1)
    spot = lax.broadcasted_iota(jnp.int32, (TOK, EXPERTS * CAP), 1).astype(F32)
    first_ref[...] = jnp.where(spot == spot_first, 1.0, 0.0).astype(BF16)
    second_ref[...] = jnp.where(spot == spot_second, 1.0, 0.0).astype(BF16)


def expert_kernel(rows_ref, inverse_ref, gate_ref, up_ref, _, out_ref):
    streams = rows_ref.shape[0]
    first_stream = pl.program_id(0) * streams
    gate = up = squares = None
    for k in range(8):
        piece = jnp.concatenate(
            [
                rows_ref[s, :, holder_of(k, first_stream + s)].reshape(128, CHUNK)
                for s in range(streams)
            ],
            axis=0,
        )
        span = slice(k * CHUNK, (k + 1) * CHUNK)
        plain = piece.astype(F32) * inverse_ref[k : k + 1, :]
        gate_k = jnp.dot(piece, gate_ref[span], preferred_element_type=F32)
        up_k = jnp.dot(piece, up_ref[span], preferred_element_type=F32)
        squares_k = plain * plain
        if k == 0:
            gate, up, squares = gate_k, up_k, squares_k
        else:
            gate, up, squares = gate + gate_k, up + up_k, squares + squares_k
    meansq = jnp.sum(squares, axis=-1, keepdims=True) * (1.0 / D)
    factor = lax.rsqrt(meansq + 1e-06)
    gate, up = gate * factor, up * factor
    active = (gate / (1.0 + jnp.exp(-gate)) * up).astype(BF16)
    width = active.shape[1]
    row = lax.broadcasted_iota(jnp.int32, (width, width), 0)
    col = lax.broadcasted_iota(jnp.int32, (width, width), 1)
    same = jnp.where(row == col, 1.0, 0.0).astype(BF16)
    for s in range(rows_ref.shape[0]):
        out_ref[s] = lax.dot_general(
            same,
            active[s * 128 : (s + 1) * 128],
            (((1,), (1,)), ((), ())),
            preferred_element_type=F32,
        ).astype(BF16)


def expert_call(rows, inverse, gate, up, after):
    step = 2
    width = gate.shape[1]
    whole = pl.BlockSpec(memory_space=pltpu.VMEM)
    return pl.pallas_call(
        expert_kernel,
        grid=(8 // step,),
        in_specs=[
            pl.BlockSpec((step, 4, 8, 2, 16, CHUNK), lambda i: (i, 0, 0, 0, 0, 0)),
            whole,
            whole,
            whole,
            pl.BlockSpec(memory_space=pl.ANY),
        ],
        out_specs=pl.BlockSpec((step, width, 128), lambda i: (i, 0, 0)),
        out_shape=jax.ShapeDtypeStruct((8, width, 128), BF16),
        compiler_params=pltpu.CompilerParams(vmem_limit_bytes=VMEM_LIMIT),
    )(rows, inverse, gate, up, after)


def down_kernel(active_ref, down_ref, out_ref):
    row = lax.broadcasted_iota(jnp.int32, (128, 128), 0)
    col = lax.broadcasted_iota(jnp.int32, (128, 128), 1)
    source = row // 32 * 32 + row // 2 % 2 * 16 + row // 4 % 8 * 2 + row % 2
    order = jnp.where(col == source, 1.0, 0.0).astype(BF16)
    hidden = active_ref.shape[0] * active_ref.shape[1]
    active = lax.dot_general(
        order,
        active_ref[...].reshape(hidden, 128),
        (((1,), (1,)), ((), ())),
        preferred_element_type=F32,
    ).astype(BF16)
    for k in range(4):
        cols = slice(k * 512, (k + 1) * 512)
        down = down_ref[:, :, cols].reshape(hidden, 512)
        out_ref[:, cols] = jnp.dot(active, down, preferred_element_type=F32).astype(BF16)


def combine_kernel(hidden_ref, gates_ref, first_ref, second_ref, rows_ref, out_ref):
    rows = rows_ref[...]
    first = jnp.dot(first_ref[...], rows, preferred_element_type=F32)
    second = jnp.dot(second_ref[...], rows, preferred_element_type=F32)
    moe = first * gates_ref[:, 0:1] + second * gates_ref[:, 1:2]
    out_ref[...] = (hidden_ref[...] + moe).astype(BF16)


def shards(
    residual,
    queries,
    keys,
    values,
    block_mask,
    out_weight,
    norm_gain,
    router,
    route_ids,
    w_gate,
    w_up,
    w_down,
):
    seq = ("x", "z", "c")
    place = jnp.stack([lax.axis_index(a) for a in ("x", "z", "c", "y")]).astype(jnp.int32)
    ids = route_ids[0]
    shape = lambda *s: jax.ShapeDtypeStruct(s, BF16)
    swap = lambda a, axes: lax.all_to_all(a, axes, split_axis=0, concat_axis=0, tiled=True)

    down = lax.all_gather(w_down[0], "y", axis=0)
    share = out_weight.shape[0] // 4
    quarter = lax.axis_index("x") % 2 * 2 + lax.axis_index("c")
    weight = lax.dynamic_slice_in_dim(out_weight, quarter * share, share, axis=0)
    weight = lax.ppermute(
        weight, ("z", "y"), [(z * 8 + y, z * 8 + (z - y) % 8) for z in range(8) for y in range(8)]
    )

    packed = vmem_call(
        pack_kernel,
        shape(8, 176, HEAD),
        6,
        smem=(0,),
        hbm=(1, 2, 3, 4, 5),
        scratch=(
            *(pltpu.VMEM((TOK, 8 * HEAD), BF16) for _ in range(3)),
            pltpu.VMEM((TOK, D), BF16),
            pltpu.VMEM((2, TOK), jnp.int32),
            pltpu.SemaphoreType.DMA((5,)),
        ),
        limit=60 * 1024 * 1024,
    )(place, queries[0], keys[0], values[0], residual[0], ids.T)
    packed = swap(packed, "z")
    kv = vmem_call(spread_kernel, shape(8, 8, 2 * TOK, HEAD), 1)(packed)
    kv = swap(kv, ("x", "c"))
    att = vmem_call(attend_kernel, shape(8, 8 * TOK, HEAD), 5, smem=(0,), hbm=(4,))(
        place, block_mask[0], packed, kv.reshape(64, 2 * TOK, HEAD), weight
    )
    other_core = [(0, 1), (1, 0)]
    beside = lax.ppermute(weight, "x", [(0, 1), (1, 0), (2, 3), (3, 2)])
    weights = (
        weight, lax.ppermute(weight, "c", other_core), beside, lax.ppermute(beside, "c", other_core)
    )
    att = swap(att, "z")
    attended, projected, buffer = vmem_call(
        project_kernel,
        (shape(TOK, 8 * HEAD), shape(8, TOK, CHUNK), shape(EXPERTS, 16, CHUNK)),
        8,
        smem=(0,),
    )(place, att, *weights, packed, norm_gain.reshape(8, CHUNK))

    arrived = swap(buffer, seq) + down[0, 0, 0] * 0
    rows = lax.all_gather(arrived, "y", axis=0)
    projected = swap(projected, "z")
    hidden, gates, first, second = vmem_call(
        gates_kernel,
        (
            jax.ShapeDtypeStruct((TOK, D), F32),
            jax.ShapeDtypeStruct((TOK, 2), F32),
            shape(TOK, EXPERTS * CAP),
            shape(TOK, EXPERTS * CAP),
        ),
        6,
        smem=(0,),
    )(place, projected, residual[0], norm_gain[None], router, ids)

    active = expert_call(
        rows.reshape(8, 4, 8, 2, 16, CHUNK),
        (1.0 / norm_gain).reshape(8, CHUNK),
        w_gate[0],
        w_up[0],
        gates,
    )
    out = vmem_call(down_kernel, shape(128, D), 2)(swap(active, "y"), down)
    returned = swap(out.reshape(EXPERTS, CAP, D), seq)
    mixed = vmem_call(combine_kernel, shape(TOK, D), 5)(
        hidden, gates, first, second, returned.reshape(EXPERTS * CAP, D)
    )
    return (attended[None], mixed[None])


def solution(mesh):
    mesh = Mesh(mesh.devices.reshape(4, 8, 2, 8), ("x", "z", "c", "y"))
    seq = ("x", "z", "c")
    placed = (
        P("y", seq, None),
        P("y", seq, None),
        P("y", seq, None),
        P("y", seq, None),
        P("y", None, None),
        P(None, "y"),
        P(),
        P(),
        P("y", seq, None),
        P(seq, None, "y"),
        P(seq, None, "y"),
        P(seq, "y", None),
    )
    return jax.shard_map(
        shards,
        mesh=mesh,
        in_specs=placed,
        out_specs=(P("y", seq, None), P("y", seq, None)),
        check_vma=False,
    )
```

```python
import jax
import jax.numpy as jnp
from jax import lax
from jax.experimental import pallas as pl
from jax.experimental.pallas import tpu as pltpu
from jax.sharding import Mesh
from jax.sharding import PartitionSpec as P

HEAD = 128
CAP = 2
BLOCK = 128
TOK = 32
D = 2048
CHUNK = 256
EXPERTS = 64
F32 = jnp.float32
BF16 = jnp.bfloat16
VMEM_LIMIT = 32 * 1024 * 1024


def vmem_call(body, out_shape, n_in, hbm=(), unread=(), scratch=(), limit=VMEM_LIMIT, flops=0):
    space = lambda i: pltpu.HBM if i in hbm else pl.ANY if i in unread else pltpu.VMEM
    return pl.pallas_call(
        body,
        out_shape=out_shape,
        in_specs=[pl.BlockSpec(memory_space=space(i)) for i in range(n_in)],
        out_specs=jax.tree.map(lambda _: pl.BlockSpec(memory_space=pltpu.VMEM), out_shape),
        scratch_shapes=list(scratch),
        cost_estimate=pl.CostEstimate(flops=flops, bytes_accessed=flops // 512, transcendentals=0),
        compiler_params=pltpu.CompilerParams(vmem_limit_bytes=limit),
    )


def slot_spots(ids):
    expert = lax.broadcasted_iota(jnp.int32, (TOK, EXPERTS), 1)
    first = jnp.where(expert == ids[:, 0:1], 1.0, 0.0)
    second = jnp.where(expert == ids[:, 1:2], 1.0, 0.0)
    row = lax.broadcasted_iota(jnp.int32, (TOK, TOK), 0)
    col = lax.broadcasted_iota(jnp.int32, (TOK, TOK), 1)
    lower = jnp.where(row > col, 1.0, 0.0).astype(BF16)
    earlier = jnp.dot(lower, (first + second).astype(BF16), preferred_element_type=F32)
    base = CAP * expert.astype(F32) + earlier
    spot_first = jnp.sum(first * base, axis=-1, keepdims=True)
    spot_second = jnp.sum(second * base, axis=-1, keepdims=True)
    return first, second, spot_first, spot_second


def chunk_of(z, y):
    return lax.rem(z - y + 8, 8)


def holder_of(chunk, y):
    return lax.rem(chunk + y, 8)


def pack_kernel(
    mask_ref, query_hbm, key_hbm, value_hbm, residual_hbm, ids_hbm, out_ref, mask_out_ref,
    query_ref, key_ref, value_ref, residual_ref, ids_ref, sems,
):
    pairs = (
        (ids_hbm, ids_ref), (query_hbm, query_ref), (key_hbm, key_ref), (value_hbm, value_ref),
        (residual_hbm, residual_ref),
    )
    copies = [pltpu.make_async_copy(a, b, sems.at[i]) for i, (a, b) in enumerate(pairs)]
    for copy in copies:
        copy.start()
    z, y = lax.axis_index("z"), lax.axis_index("y")
    mask_out_ref[...] = mask_ref[...]
    copies[0].wait()
    expert = lax.broadcasted_iota(jnp.int32, (EXPERTS, TOK), 0)
    first = jnp.where(expert == ids_ref[0:1], 1.0, 0.0)
    second = jnp.where(expert == ids_ref[1:2], 1.0, 0.0)
    row = lax.broadcasted_iota(jnp.int32, (TOK, TOK), 0)
    col = lax.broadcasted_iota(jnp.int32, (TOK, TOK), 1)
    upper = jnp.where(row < col, 1.0, 0.0).astype(BF16)
    earlier = jnp.dot((first + second).astype(BF16), upper, preferred_element_type=F32)
    base = CAP * expert.astype(F32) + earlier
    spot_first = jnp.sum(first * base, axis=0, keepdims=True)
    spot_second = jnp.sum(second * base, axis=0, keepdims=True)
    row = lax.broadcasted_iota(jnp.int32, (16, TOK), 0)
    tile = jnp.where(row < 2, spot_first, jnp.where(row < 4, spot_second, 0.0)).astype(BF16)
    lane = lax.broadcasted_iota(jnp.int32, (TOK, 2 * HEAD), 1)
    token = lax.broadcasted_iota(jnp.int32, (TOK, 2 * HEAD), 0)
    here = jnp.where(lane == z * TOK + token, 1.0, 0.0).astype(BF16)
    tile = jnp.dot(tile, here, preferred_element_type=F32)
    row = lax.broadcasted_iota(jnp.int32, (16, HEAD), 0)
    tile = jnp.where(row % 2 == 0, tile[:, :HEAD], tile[:, HEAD:]).astype(BF16)
    for copy in copies[1:]:
        copy.wait()
    for h in range(8):
        cols = slice(h * HEAD, (h + 1) * HEAD)
        out_ref[h, 0:32] = query_ref[:, cols]
        out_ref[h, 32:64] = key_ref[:, cols]
        out_ref[h, 64:96] = value_ref[:, cols]
        out_ref[h, 160:176] = tile
        holder = holder_of(h, y)
        out_ref[holder, 96:128] = residual_ref[:, h * CHUNK : h * CHUNK + HEAD]
        out_ref[holder, 128:160] = residual_ref[:, h * CHUNK + HEAD : (h + 1) * CHUNK]


def spread_kernel(packed_ref, _, out_ref):
    for i in range(4):
        out_ref[i] = packed_ref[:, 32:96]


def attend_kernel(mask_ref, packed_ref, own_ref, other_ref, out_ref):
    x, c = lax.axis_index("x"), lax.axis_index("c")
    refs = (own_ref, other_ref)
    n_key = 2 * own_ref.shape[0] * TOK
    keys = jnp.concatenate([ref[:, :TOK].reshape(n_key // 2, HEAD) for ref in refs], axis=0)
    values = jnp.concatenate([ref[:, TOK:].reshape(n_key // 2, HEAD) for ref in refs], axis=0)
    key_row = lax.broadcasted_iota(jnp.int32, (1, n_key), 1)
    key_x, key_z, key_t = key_row // 256 % 4, key_row // 32 % 8, key_row % 32
    key_c = jnp.where(key_row < n_key // 2, c, 1 - c)
    key_pos = key_x * 512 + key_z * 64 + key_c * 32 + key_t
    block_row = lax.broadcasted_iota(jnp.int32, (16, n_key), 0)
    key_onehot = (block_row == jnp.broadcast_to(key_pos // BLOCK, (16, n_key))).astype(BF16)
    row_i = lax.broadcasted_iota(jnp.int32, (16, 16), 0)
    col_i = lax.broadcasted_iota(jnp.int32, (16, 16), 1)
    live = ((mask_ref[...] > 0) | (row_i == col_i)).astype(BF16)
    seen = jnp.dot(live, key_onehot, preferred_element_type=F32)
    seen_row = lax.broadcasted_iota(jnp.int32, (16, n_key), 0)
    scale = HEAD ** (-0.5)
    for j in range(4):
        mine = jnp.sum(jnp.where(seen_row == x * 4 + j, seen, 0.0), axis=0, keepdims=True)
        rows = packed_ref[2 * j : 2 * j + 2, :TOK].reshape(2 * TOK, HEAD)
        row = lax.broadcasted_iota(jnp.int32, (2 * TOK, 1), 0)
        query_pos = x * 512 + (2 * j + row // 32) * 64 + c * 32 + row % 32
        allowed = (jnp.broadcast_to(mine, (2 * TOK, n_key)) > 0.5) & (key_pos <= query_pos)
        scores = lax.dot_general(rows, keys, (((1,), (1,)), ((), ())), preferred_element_type=F32)
        scores = jnp.where(allowed, scores * scale, -1e30)
        top = jnp.max(scores, axis=-1, keepdims=True)
        weights = jnp.exp(scores - top)
        total = jnp.sum(weights, axis=-1, keepdims=True)
        update = jnp.dot(weights.astype(BF16), values, preferred_element_type=F32)
        attended = (update / total).astype(BF16)
        for z in range(8):
            out_ref[z, 2 * j * TOK : 2 * (j + 1) * TOK] = attended


def route_kernel(packed_ref, out_ref):
    spots = jnp.sum(packed_ref[:, 160:176].astype(F32), axis=0)
    spot_first = jnp.concatenate([spots[0:1], spots[1:2]], axis=1)
    spot_second = jnp.concatenate([spots[2:3], spots[3:4]], axis=1)
    row = lax.broadcasted_iota(jnp.int32, (8 * EXPERTS * CAP, 1), 0)
    row_spot = (row // 16 * CAP + row % CAP).astype(F32)
    row_block = row // CAP % 8
    col_block = lax.broadcasted_iota(jnp.int32, (1, 8 * TOK), 1) // TOK
    taken = (spot_first == row_spot) | (spot_second == row_spot)
    out_ref[...] = jnp.where(taken & (row_block == col_block), 1.0, 0.0).astype(BF16)


def project_kernel(
    att_ref, own_ref, core_ref, x_ref, x_core_ref, packed_ref, gain_ref, route_ref,
    attended_ref, projected_ref, buffer_ref,
):
    z, y = lax.axis_index("z"), lax.axis_index("y")
    mine = pl.ds(pl.multiple_of(z * TOK, TOK), TOK)
    attended_ref[...] = jnp.concatenate([att_ref[h, mine] for h in range(8)], axis=1)
    quarter = lax.axis_index("x") % 2 * 2 + lax.axis_index("c")
    total = None
    for ref, flip in ((own_ref, 0), (core_ref, 1), (x_ref, 2), (x_core_ref, 3)):
        rows = quarter ^ flip
        attended = jnp.concatenate([att_ref[2 * rows], att_ref[2 * rows + 1]], axis=1)
        part = jnp.dot(attended, ref[...], preferred_element_type=F32)
        total = part if total is None else total + part
    projected = total.astype(BF16)
    projected_ref[...] = projected.reshape(8, TOK, CHUNK)
    residual = jnp.concatenate(
        [packed_ref[:, 96:128].reshape(8 * TOK, HEAD), packed_ref[:, 128:160].reshape(8 * TOK, HEAD)],
        axis=1,
    )
    hidden = residual.astype(F32) + projected.astype(F32)
    scaled = (hidden * gain_ref[pl.ds(chunk_of(z, y), 1), :]).astype(BF16)
    rows = jnp.dot(route_ref[...], scaled, preferred_element_type=F32).astype(BF16)
    buffer_ref[...] = rows.reshape(EXPERTS, 16, CHUNK)


def gates_kernel(
    projected_ref, residual_ref, gain_ref, router_ref, ids_ref, down_hbm,
    hidden_ref, gates_ref, first_ref, second_ref, down_ref, sem,
):
    copy = pltpu.make_async_copy(down_hbm, down_ref, sem)
    copy.start()
    y = lax.axis_index("y")
    projected = jnp.concatenate([projected_ref[holder_of(k, y)] for k in range(8)], axis=1)
    hidden = residual_ref[...].astype(F32) + projected.astype(F32)
    hidden_ref[...] = hidden
    meansq = jnp.mean(hidden * hidden, axis=-1, keepdims=True)
    normed = (hidden * lax.rsqrt(meansq + 1e-06) * gain_ref[...]).astype(BF16)
    logits = jnp.dot(normed, router_ref[...], preferred_element_type=F32)
    first, second, spot_first, spot_second = slot_spots(ids_ref[...])
    logit_first = jnp.sum(first * logits, axis=-1, keepdims=True)
    logit_second = jnp.sum(second * logits, axis=-1, keepdims=True)
    gate = jax.nn.sigmoid(logit_first - logit_second)
    gates_ref[...] = jnp.concatenate([gate, 1.0 - gate], axis=1)
    spot = lax.broadcasted_iota(jnp.int32, (TOK, EXPERTS * CAP), 1).astype(F32)
    first_ref[...] = jnp.where(spot == spot_first, 1.0, 0.0).astype(BF16)
    second_ref[...] = jnp.where(spot == spot_second, 1.0, 0.0).astype(BF16)
    copy.wait()


def expert_kernel(rows_ref, inverse_ref, weight_ref, _, out_ref):
    transposed = (((1,), (1,)), ((), ()))
    streams = rows_ref.shape[0]
    first_stream = pl.program_id(0) * streams
    units = squares = None
    for k in range(8):
        piece = jnp.concatenate(
            [
                rows_ref[s, :, holder_of(k, first_stream + s)].reshape(128, CHUNK)
                for s in range(streams)
            ],
            axis=0,
        )
        plain = piece.astype(F32) * inverse_ref[k : k + 1, :]
        weight = weight_ref[:, k * CHUNK : (k + 1) * CHUNK]
        part = lax.dot_general(weight, piece, transposed, preferred_element_type=F32)
        units = part if k == 0 else units + part
        squares = plain * plain if k == 0 else squares + plain * plain
    high = squares.astype(BF16)
    low = (squares - high.astype(F32)).astype(BF16)
    ones = jnp.ones((16, CHUNK), BF16)
    sums = [lax.dot_general(ones, a, transposed, preferred_element_type=F32) for a in (high, low)]
    factor = lax.rsqrt((sums[0] + sums[1])[0:1] * (1.0 / D) + 1e-06)
    units = units * factor
    width = units.shape[0] // 2
    gate, up = units[:width], units[width:]
    active = (gate / (1.0 + jnp.exp(-gate)) * up).astype(BF16)
    for s in range(streams):
        out_ref[s] = active[:, s * 128 : (s + 1) * 128]


def expert_call(rows, inverse, weight, after):
    step = 2
    width = weight.shape[0] // 2
    whole = pl.BlockSpec(memory_space=pltpu.VMEM)
    return pl.pallas_call(
        expert_kernel,
        grid=(8 // step,),
        in_specs=[
            pl.BlockSpec((step, 4, 8, 2, 16, CHUNK), lambda i: (i, 0, 0, 0, 0, 0)),
            whole,
            whole,
            pl.BlockSpec(memory_space=pl.ANY),
        ],
        out_specs=pl.BlockSpec((step, width, 128), lambda i: (i, 0, 0)),
        out_shape=jax.ShapeDtypeStruct((8, width, 128), BF16),
        compiler_params=pltpu.CompilerParams(vmem_limit_bytes=48 * 1024 * 1024),
    )(rows, inverse, weight, after)


def down_kernel(active_ref, down_ref, out_ref):
    row = lax.broadcasted_iota(jnp.int32, (128, 128), 0)
    col = lax.broadcasted_iota(jnp.int32, (128, 128), 1)
    source = row // 32 * 32 + row // 2 % 2 * 16 + row // 4 % 8 * 2 + row % 2
    order = jnp.where(col == source, 1.0, 0.0).astype(BF16)
    hidden = active_ref.shape[0] * active_ref.shape[1]
    active = lax.dot_general(
        order,
        active_ref[...].reshape(hidden, 128),
        (((1,), (1,)), ((), ())),
        preferred_element_type=F32,
    ).astype(BF16)
    for k in range(4):
        cols = slice(k * 512, (k + 1) * 512)
        down = down_ref[:, :, cols].reshape(hidden, 512)
        out_ref[:, cols] = jnp.dot(active, down, preferred_element_type=F32).astype(BF16)


def combine_kernel(hidden_ref, gates_ref, first_ref, second_ref, rows_ref, out_ref):
    rows = rows_ref[...]
    first = jnp.dot(first_ref[...], rows, preferred_element_type=F32)
    second = jnp.dot(second_ref[...], rows, preferred_element_type=F32)
    moe = first * gates_ref[:, 0:1] + second * gates_ref[:, 1:2]
    out_ref[...] = (hidden_ref[...] + moe).astype(BF16)


def shards(
    residual,
    queries,
    keys,
    values,
    block_mask,
    out_weight,
    norm_gain,
    router,
    route_ids,
    w_gate,
    w_up,
    w_down,
):
    seq = ("x", "z", "c")
    ids = route_ids[0]
    shape = lambda *s: jax.ShapeDtypeStruct(s, BF16)
    swap = lambda a, axes: lax.all_to_all(a, axes, split_axis=0, concat_axis=0, tiled=True)

    down = lax.all_gather(w_down[0], "y", axis=0)
    share = out_weight.shape[0] // 4
    quarter = lax.axis_index("x") % 2 * 2 + lax.axis_index("c")
    weight = lax.dynamic_slice_in_dim(out_weight, quarter * share, share, axis=0)
    weight = lax.ppermute(
        weight, ("z", "y"), [(z * 8 + y, z * 8 + (z - y) % 8) for z in range(8) for y in range(8)]
    )

    packed, mask = vmem_call(
        pack_kernel,
        (shape(8, 176, HEAD), jax.ShapeDtypeStruct(block_mask.shape[1:], jnp.int32)),
        6,
        hbm=(1, 2, 3, 4, 5),
        scratch=(
            *(pltpu.VMEM((TOK, 8 * HEAD), BF16) for _ in range(3)),
            pltpu.VMEM((TOK, D), BF16),
            pltpu.VMEM((2, TOK), jnp.int32),
            pltpu.SemaphoreType.DMA((5,)),
        ),
        limit=60 * 1024 * 1024,
    )(block_mask[0], queries[0], keys[0], values[0], residual[0], ids.T)
    packed = swap(packed, "z")
    other_core = [(0, 1), (1, 0)]
    kv = vmem_call(spread_kernel, shape(4, 8, 2 * TOK, HEAD), 2, unread=(1,))(packed, weight)
    kv = swap(kv, "x").reshape(32, 2 * TOK, HEAD)
    other_kv = lax.ppermute(kv, "c", other_core)
    att = vmem_call(attend_kernel, shape(8, 8 * TOK, HEAD), 4)(mask, packed, kv, other_kv)
    beside = lax.ppermute(weight, "x", [(0, 1), (1, 0), (2, 3), (3, 2)])
    weights = (
        weight, lax.ppermute(weight, "c", other_core), beside, lax.ppermute(beside, "c", other_core)
    )
    att = swap(att, "z")
    route = vmem_call(route_kernel, shape(8 * EXPERTS * CAP, 8 * TOK), 1, flops=2_000_000_000)(packed)
    attended, projected, buffer = vmem_call(
        project_kernel,
        (shape(TOK, 8 * HEAD), shape(8, TOK, CHUNK), shape(EXPERTS, 16, CHUNK)),
        8,
    )(att, *weights, packed, norm_gain.reshape(8, CHUNK), route)

    arrived = swap(buffer, seq) + down[0, 0, 0] * 0
    rows = lax.all_gather(arrived, "y", axis=0)
    projected = swap(projected, "z")
    hidden, gates, first, second, down = vmem_call(
        gates_kernel,
        (
            jax.ShapeDtypeStruct((TOK, D), F32),
            jax.ShapeDtypeStruct((TOK, 2), F32),
            shape(TOK, EXPERTS * CAP),
            shape(TOK, EXPERTS * CAP),
            shape(*down.shape),
        ),
        6,
        hbm=(5,),
        scratch=(pltpu.SemaphoreType.DMA(()),),
    )(projected, residual[0], norm_gain[None], router, ids, down)

    active = expert_call(
        rows.reshape(8, 4, 8, 2, 16, CHUNK),
        (1.0 / norm_gain).reshape(8, CHUNK),
        jnp.concatenate([w_gate[0].T, w_up[0].T], axis=0),
        gates,
    )
    out = vmem_call(down_kernel, shape(128, D), 2)(swap(active, "y"), down)
    returned = swap(out.reshape(EXPERTS, CAP, D), seq)
    mixed = vmem_call(combine_kernel, shape(TOK, D), 5)(
        hidden, gates, first, second, returned.reshape(EXPERTS * CAP, D)
    )
    return (attended[None], mixed[None])


def solution(mesh):
    mesh = Mesh(mesh.devices.reshape(4, 8, 2, 8), ("x", "z", "c", "y"))
    seq = ("x", "z", "c")
    placed = (
        P("y", seq, None),
        P("y", seq, None),
        P("y", seq, None),
        P("y", seq, None),
        P("y", None, None),
        P(None, "y"),
        P(),
        P(),
        P("y", seq, None),
        P(seq, None, "y"),
        P(seq, None, "y"),
        P(seq, "y", None),
    )
    return jax.shard_map(
        shards,
        mesh=mesh,
        in_specs=placed,
        out_specs=(P("y", seq, None), P("y", seq, None)),
        check_vma=False,
    )
```

```python
import jax
import jax.numpy as jnp
from jax import lax
from jax.experimental import pallas as pl
from jax.experimental.pallas import tpu as pltpu
from jax.sharding import Mesh
from jax.sharding import PartitionSpec as P

HEAD = 128
CAP = 2
BLOCK = 128
TOK = 32
D = 2048
CHUNK = 256
EXPERTS = 64
F32 = jnp.float32
BF16 = jnp.bfloat16
VMEM_LIMIT = 32 * 1024 * 1024


def vmem_call(body, out_shape, n_in, hbm=(), unread=(), scratch=(), limit=VMEM_LIMIT, flops=0):
    space = lambda i: pltpu.HBM if i in hbm else pl.ANY if i in unread else pltpu.VMEM
    return pl.pallas_call(
        body,
        out_shape=out_shape,
        in_specs=[pl.BlockSpec(memory_space=space(i)) for i in range(n_in)],
        out_specs=jax.tree.map(lambda _: pl.BlockSpec(memory_space=pltpu.VMEM), out_shape),
        scratch_shapes=list(scratch),
        cost_estimate=pl.CostEstimate(flops=flops, bytes_accessed=flops // 512, transcendentals=0),
        compiler_params=pltpu.CompilerParams(vmem_limit_bytes=limit),
    )


def slot_spots(ids):
    expert = lax.broadcasted_iota(jnp.int32, (TOK, EXPERTS), 1)
    first = jnp.where(expert == ids[:, 0:1], 1.0, 0.0)
    second = jnp.where(expert == ids[:, 1:2], 1.0, 0.0)
    row = lax.broadcasted_iota(jnp.int32, (TOK, TOK), 0)
    col = lax.broadcasted_iota(jnp.int32, (TOK, TOK), 1)
    lower = jnp.where(row > col, 1.0, 0.0).astype(BF16)
    earlier = jnp.dot(lower, (first + second).astype(BF16), preferred_element_type=F32)
    base = CAP * expert.astype(F32) + earlier
    spot_first = jnp.sum(first * base, axis=-1, keepdims=True)
    spot_second = jnp.sum(second * base, axis=-1, keepdims=True)
    return first, second, spot_first, spot_second


def chunk_of(z, y):
    return lax.rem(z - y + 8, 8)


def holder_of(chunk, y):
    return lax.rem(chunk + y, 8)


def pack_kernel(
    mask_ref, query_hbm, key_hbm, value_hbm, residual_hbm, ids_hbm, out_ref, mask_out_ref,
    query_ref, key_ref, value_ref, residual_ref, ids_ref, sems,
):
    pairs = (
        (ids_hbm, ids_ref), (query_hbm, query_ref), (key_hbm, key_ref), (value_hbm, value_ref),
        (residual_hbm, residual_ref),
    )
    copies = [pltpu.make_async_copy(a, b, sems.at[i]) for i, (a, b) in enumerate(pairs)]
    for copy in copies:
        copy.start()
    z, y = lax.axis_index("z"), lax.axis_index("y")
    mask_out_ref[...] = mask_ref[...]
    copies[0].wait()
    expert = lax.broadcasted_iota(jnp.int32, (EXPERTS, TOK), 0)
    first = jnp.where(expert == ids_ref[0:1], 1.0, 0.0)
    second = jnp.where(expert == ids_ref[1:2], 1.0, 0.0)
    row = lax.broadcasted_iota(jnp.int32, (TOK, TOK), 0)
    col = lax.broadcasted_iota(jnp.int32, (TOK, TOK), 1)
    upper = jnp.where(row < col, 1.0, 0.0).astype(BF16)
    earlier = jnp.dot((first + second).astype(BF16), upper, preferred_element_type=F32)
    base = CAP * expert.astype(F32) + earlier
    spot_first = jnp.sum(first * base, axis=0, keepdims=True)
    spot_second = jnp.sum(second * base, axis=0, keepdims=True)
    row = lax.broadcasted_iota(jnp.int32, (16, TOK), 0)
    tile = jnp.where(row < 2, spot_first, jnp.where(row < 4, spot_second, 0.0)).astype(BF16)
    lane = lax.broadcasted_iota(jnp.int32, (TOK, 2 * HEAD), 1)
    token = lax.broadcasted_iota(jnp.int32, (TOK, 2 * HEAD), 0)
    here = jnp.where(lane == z * TOK + token, 1.0, 0.0).astype(BF16)
    tile = jnp.dot(tile, here, preferred_element_type=F32)
    row = lax.broadcasted_iota(jnp.int32, (16, HEAD), 0)
    tile = jnp.where(row % 2 == 0, tile[:, :HEAD], tile[:, HEAD:]).astype(BF16)
    for copy in copies[1:]:
        copy.wait()
    for h in range(8):
        cols = slice(h * HEAD, (h + 1) * HEAD)
        out_ref[h, 0:32] = query_ref[:, cols]
        out_ref[h, 32:64] = key_ref[:, cols]
        out_ref[h, 64:96] = value_ref[:, cols]
        out_ref[h, 160:176] = tile
        holder = holder_of(h, y)
        out_ref[holder, 96:128] = residual_ref[:, h * CHUNK : h * CHUNK + HEAD]
        out_ref[holder, 128:160] = residual_ref[:, h * CHUNK + HEAD : (h + 1) * CHUNK]


def spread_kernel(packed_ref, _, out_ref):
    for i in range(4):
        out_ref[i] = packed_ref[:, 32:96]


def attend_kernel(mask_ref, packed_ref, own_ref, other_ref, out_ref):
    x, c = lax.axis_index("x"), lax.axis_index("c")
    refs = (own_ref, other_ref)
    n_key = 2 * own_ref.shape[0] * TOK
    keys = jnp.concatenate([ref[:, :TOK].reshape(n_key // 2, HEAD) for ref in refs], axis=0)
    values = jnp.concatenate([ref[:, TOK:].reshape(n_key // 2, HEAD) for ref in refs], axis=0)
    key_row = lax.broadcasted_iota(jnp.int32, (1, n_key), 1)
    key_x, key_z, key_t = key_row // 256 % 4, key_row // 32 % 8, key_row % 32
    key_c = jnp.where(key_row < n_key // 2, c, 1 - c)
    key_pos = key_x * 512 + key_z * 64 + key_c * 32 + key_t
    block_row = lax.broadcasted_iota(jnp.int32, (16, n_key), 0)
    key_onehot = (block_row == jnp.broadcast_to(key_pos // BLOCK, (16, n_key))).astype(BF16)
    row_i = lax.broadcasted_iota(jnp.int32, (16, 16), 0)
    col_i = lax.broadcasted_iota(jnp.int32, (16, 16), 1)
    live = ((mask_ref[...] > 0) | (row_i == col_i)).astype(BF16)
    seen = jnp.dot(live, key_onehot, preferred_element_type=F32)
    seen_row = lax.broadcasted_iota(jnp.int32, (16, n_key), 0)
    scale = HEAD ** (-0.5)
    mine = [
        jnp.sum(jnp.where(seen_row == x * 4 + j, seen, 0.0), axis=0, keepdims=True) for j in range(4)
    ]
    mine = jnp.concatenate([jnp.broadcast_to(m, (2 * TOK, n_key)) for m in mine], axis=0)
    rows = packed_ref[:, :TOK].reshape(8 * TOK, HEAD)
    row = lax.broadcasted_iota(jnp.int32, (8 * TOK, 1), 0)
    query_pos = x * 512 + row // 32 * 64 + c * 32 + row % 32
    allowed = (mine > 0.5) & (key_pos <= query_pos)
    scores = lax.dot_general(rows, keys, (((1,), (1,)), ((), ())), preferred_element_type=F32)
    scores = jnp.where(allowed, scores * scale, -1e30)
    top = jnp.max(scores, axis=-1, keepdims=True)
    weights = jnp.exp(scores - top)
    total = jnp.sum(weights, axis=-1, keepdims=True)
    update = jnp.dot(weights.astype(BF16), values, preferred_element_type=F32)
    attended = (update / total).astype(BF16)
    for z in range(8):
        out_ref[z] = attended


def route_kernel(packed_ref, out_ref):
    spots = jnp.sum(packed_ref[:, 160:176].astype(F32), axis=0)
    spot_first = jnp.concatenate([spots[0:1], spots[1:2]], axis=1)
    spot_second = jnp.concatenate([spots[2:3], spots[3:4]], axis=1)
    row = lax.broadcasted_iota(jnp.int32, (8 * EXPERTS * CAP, 1), 0)
    row_spot = (row // 16 * CAP + row % CAP).astype(F32)
    row_block = row // CAP % 8
    col_block = lax.broadcasted_iota(jnp.int32, (1, 8 * TOK), 1) // TOK
    taken = (spot_first == row_spot) | (spot_second == row_spot)
    out_ref[...] = jnp.where(taken & (row_block == col_block), 1.0, 0.0).astype(BF16)


def project_kernel(
    att_ref, own_ref, core_ref, x_ref, x_core_ref, packed_ref, gain_ref, route_ref,
    attended_ref, projected_ref, buffer_ref,
):
    z, y = lax.axis_index("z"), lax.axis_index("y")
    mine = pl.ds(pl.multiple_of(z * TOK, TOK), TOK)
    attended_ref[...] = jnp.concatenate([att_ref[h, mine] for h in range(8)], axis=1)
    quarter = lax.axis_index("x") % 2 * 2 + lax.axis_index("c")
    total = None
    for ref, flip in ((own_ref, 0), (core_ref, 1), (x_ref, 2), (x_core_ref, 3)):
        rows = quarter ^ flip
        attended = jnp.concatenate([att_ref[2 * rows], att_ref[2 * rows + 1]], axis=1)
        part = jnp.dot(attended, ref[...], preferred_element_type=F32)
        total = part if total is None else total + part
    projected = total.astype(BF16)
    projected_ref[...] = projected.reshape(8, TOK, CHUNK)
    residual = jnp.concatenate(
        [packed_ref[:, 96:128].reshape(8 * TOK, HEAD), packed_ref[:, 128:160].reshape(8 * TOK, HEAD)],
        axis=1,
    )
    hidden = residual.astype(F32) + projected.astype(F32)
    scaled = (hidden * gain_ref[pl.ds(chunk_of(z, y), 1), :]).astype(BF16)
    rows = jnp.dot(route_ref[...], scaled, preferred_element_type=F32).astype(BF16)
    buffer_ref[...] = rows.reshape(EXPERTS, 16, CHUNK)


def gates_kernel(
    projected_ref, residual_ref, gain_ref, router_ref, ids_ref, down_hbm,
    hidden_ref, gates_ref, first_ref, second_ref, down_ref, sem,
):
    copy = pltpu.make_async_copy(down_hbm, down_ref, sem)
    copy.start()
    y = lax.axis_index("y")
    projected = jnp.concatenate([projected_ref[holder_of(k, y)] for k in range(8)], axis=1)
    hidden = residual_ref[...].astype(F32) + projected.astype(F32)
    hidden_ref[...] = hidden
    meansq = jnp.mean(hidden * hidden, axis=-1, keepdims=True)
    normed = (hidden * lax.rsqrt(meansq + 1e-06) * gain_ref[...]).astype(BF16)
    logits = jnp.dot(normed, router_ref[...], preferred_element_type=F32)
    first, second, spot_first, spot_second = slot_spots(ids_ref[...])
    logit_first = jnp.sum(first * logits, axis=-1, keepdims=True)
    logit_second = jnp.sum(second * logits, axis=-1, keepdims=True)
    gate = jax.nn.sigmoid(logit_first - logit_second)
    gates_ref[...] = jnp.concatenate([gate, 1.0 - gate], axis=1)
    spot = lax.broadcasted_iota(jnp.int32, (TOK, EXPERTS * CAP), 1).astype(F32)
    first_ref[...] = jnp.where(spot == spot_first, 1.0, 0.0).astype(BF16)
    second_ref[...] = jnp.where(spot == spot_second, 1.0, 0.0).astype(BF16)
    copy.wait()


def expert_kernel(rows_ref, inverse_ref, weight_ref, _, out_ref):
    transposed = (((1,), (1,)), ((), ()))
    streams = rows_ref.shape[0]
    first_stream = pl.program_id(0) * streams
    units = squares = None
    for k in range(8):
        piece = jnp.concatenate(
            [
                rows_ref[s, :, holder_of(k, first_stream + s)].reshape(128, CHUNK)
                for s in range(streams)
            ],
            axis=0,
        )
        plain = piece.astype(F32) * inverse_ref[k : k + 1, :]
        weight = weight_ref[:, k * CHUNK : (k + 1) * CHUNK]
        part = lax.dot_general(weight, piece, transposed, preferred_element_type=F32)
        units = part if k == 0 else units + part
        squares = plain * plain if k == 0 else squares + plain * plain
    high = squares.astype(BF16)
    low = (squares - high.astype(F32)).astype(BF16)
    ones = jnp.ones((16, CHUNK), BF16)
    sums = [lax.dot_general(ones, a, transposed, preferred_element_type=F32) for a in (high, low)]
    factor = lax.rsqrt((sums[0] + sums[1])[0:1] * (1.0 / D) + 1e-06)
    units = units * factor
    width = units.shape[0] // 2
    gate, up = units[:width], units[width:]
    active = (gate / (1.0 + jnp.exp(-gate)) * up).astype(BF16)
    for s in range(streams):
        out_ref[s] = active[:, s * 128 : (s + 1) * 128]


def expert_call(rows, inverse, weight, after):
    step = 2
    width = weight.shape[0] // 2
    whole = pl.BlockSpec(memory_space=pltpu.VMEM)
    return pl.pallas_call(
        expert_kernel,
        grid=(8 // step,),
        in_specs=[
            pl.BlockSpec((step, 4, 8, 2, 16, CHUNK), lambda i: (i, 0, 0, 0, 0, 0)),
            whole,
            whole,
            pl.BlockSpec(memory_space=pl.ANY),
        ],
        out_specs=pl.BlockSpec((step, width, 128), lambda i: (i, 0, 0)),
        out_shape=jax.ShapeDtypeStruct((8, width, 128), BF16),
        compiler_params=pltpu.CompilerParams(vmem_limit_bytes=51 * 1024 * 1024),
    )(rows, inverse, weight, after)


def down_kernel(active_ref, down_ref, out_ref):
    row = lax.broadcasted_iota(jnp.int32, (128, 128), 0)
    col = lax.broadcasted_iota(jnp.int32, (128, 128), 1)
    source = row // 32 * 32 + row // 2 % 2 * 16 + row // 4 % 8 * 2 + row % 2
    order = jnp.where(col == source, 1.0, 0.0).astype(BF16)
    hidden = active_ref.shape[0] * active_ref.shape[1]
    active = lax.dot_general(
        order,
        active_ref[...].reshape(hidden, 128),
        (((1,), (1,)), ((), ())),
        preferred_element_type=F32,
    ).astype(BF16)
    for k in range(4):
        cols = slice(k * 512, (k + 1) * 512)
        down = down_ref[:, :, cols].reshape(hidden, 512)
        out_ref[:, cols] = jnp.dot(active, down, preferred_element_type=F32).astype(BF16)


def combine_kernel(hidden_ref, gates_ref, first_ref, second_ref, rows_ref, out_ref):
    rows = rows_ref[...]
    first = jnp.dot(first_ref[...], rows, preferred_element_type=F32)
    second = jnp.dot(second_ref[...], rows, preferred_element_type=F32)
    moe = first * gates_ref[:, 0:1] + second * gates_ref[:, 1:2]
    out_ref[...] = (hidden_ref[...] + moe).astype(BF16)


def shards(
    residual,
    queries,
    keys,
    values,
    block_mask,
    out_weight,
    norm_gain,
    router,
    route_ids,
    w_gate,
    w_up,
    w_down,
):
    seq = ("x", "z", "c")
    ids = route_ids[0]
    shape = lambda *s: jax.ShapeDtypeStruct(s, BF16)
    swap = lambda a, axes: lax.all_to_all(a, axes, split_axis=0, concat_axis=0, tiled=True)

    down = lax.all_gather(w_down[0], "y", axis=0)
    share = out_weight.shape[0] // 4
    quarter = lax.axis_index("x") % 2 * 2 + lax.axis_index("c")
    weight = lax.dynamic_slice_in_dim(out_weight, quarter * share, share, axis=0)
    weight = lax.ppermute(
        weight, ("z", "y"), [(z * 8 + y, z * 8 + (z - y) % 8) for z in range(8) for y in range(8)]
    )

    packed, mask = vmem_call(
        pack_kernel,
        (shape(8, 176, HEAD), jax.ShapeDtypeStruct(block_mask.shape[1:], jnp.int32)),
        6,
        hbm=(1, 2, 3, 4, 5),
        scratch=(
            *(pltpu.VMEM((TOK, 8 * HEAD), BF16) for _ in range(3)),
            pltpu.VMEM((TOK, D), BF16),
            pltpu.VMEM((2, TOK), jnp.int32),
            pltpu.SemaphoreType.DMA((5,)),
        ),
        limit=60 * 1024 * 1024,
    )(block_mask[0], queries[0], keys[0], values[0], residual[0], ids.T)
    packed = swap(packed, "z")
    other_core = [(0, 1), (1, 0)]
    kv = vmem_call(spread_kernel, shape(4, 8, 2 * TOK, HEAD), 2, unread=(1,))(packed, weight)
    kv = swap(kv, "x").reshape(32, 2 * TOK, HEAD)
    other_kv = lax.ppermute(kv, "c", other_core)
    att = vmem_call(attend_kernel, shape(8, 8 * TOK, HEAD), 4)(mask, packed, kv, other_kv)
    beside = lax.ppermute(weight, "x", [(0, 1), (1, 0), (2, 3), (3, 2)])
    weights = (
        weight, lax.ppermute(weight, "c", other_core), beside, lax.ppermute(beside, "c", other_core)
    )
    att = swap(att, "z")
    route = vmem_call(route_kernel, shape(8 * EXPERTS * CAP, 8 * TOK), 1, flops=2_000_000_000)(packed)
    attended, projected, buffer = vmem_call(
        project_kernel,
        (shape(TOK, 8 * HEAD), shape(8, TOK, CHUNK), shape(EXPERTS, 16, CHUNK)),
        8,
    )(att, *weights, packed, norm_gain.reshape(8, CHUNK), route)

    arrived = swap(buffer, seq) + down[0, 0, 0] * 0
    rows = lax.all_gather(arrived, "y", axis=0)
    projected = swap(projected, "z")
    hidden, gates, first, second, down = vmem_call(
        gates_kernel,
        (
            jax.ShapeDtypeStruct((TOK, D), F32),
            jax.ShapeDtypeStruct((TOK, 2), F32),
            shape(TOK, EXPERTS * CAP),
            shape(TOK, EXPERTS * CAP),
            shape(*down.shape),
        ),
        6,
        hbm=(5,),
        scratch=(pltpu.SemaphoreType.DMA(()),),
    )(projected, residual[0], norm_gain[None], router, ids, down)

    active = expert_call(
        rows.reshape(8, 4, 8, 2, 16, CHUNK),
        (1.0 / norm_gain).reshape(8, CHUNK),
        jnp.concatenate([w_gate[0].T, w_up[0].T], axis=0),
        gates,
    )
    out = vmem_call(down_kernel, shape(128, D), 2)(swap(active, "y"), down)
    returned = swap(out.reshape(EXPERTS, CAP, D), seq)
    mixed = vmem_call(combine_kernel, shape(TOK, D), 5)(
        hidden, gates, first, second, returned.reshape(EXPERTS * CAP, D)
    )
    return (attended[None], mixed[None])


def solution(mesh):
    mesh = Mesh(mesh.devices.reshape(4, 8, 2, 8), ("x", "z", "c", "y"))
    seq = ("x", "z", "c")
    placed = (
        P("y", seq, None),
        P("y", seq, None),
        P("y", seq, None),
        P("y", seq, None),
        P("y", None, None),
        P(None, "y"),
        P(),
        P(),
        P("y", seq, None),
        P(seq, None, "y"),
        P(seq, None, "y"),
        P(seq, "y", None),
    )
    return jax.shard_map(
        shards,
        mesh=mesh,
        in_specs=placed,
        out_specs=(P("y", seq, None), P("y", seq, None)),
        check_vma=False,
    )
```

```python
import jax
import jax.numpy as jnp
from jax import lax
from jax.experimental import pallas as pl
from jax.experimental.pallas import tpu as pltpu
from jax.sharding import Mesh
from jax.sharding import PartitionSpec as P

HEAD = 128
CAP = 2
BLOCK = 128
TOK = 32
D = 2048
CHUNK = 256
EXPERTS = 64
F32 = jnp.float32
BF16 = jnp.bfloat16
VMEM_LIMIT = 32 * 1024 * 1024


def vmem_call(body, out_shape, n_in, hbm=(), unread=(), scratch=(), limit=VMEM_LIMIT, flops=0):
    space = lambda i: pltpu.HBM if i in hbm else pl.ANY if i in unread else pltpu.VMEM
    return pl.pallas_call(
        body,
        out_shape=out_shape,
        in_specs=[pl.BlockSpec(memory_space=space(i)) for i in range(n_in)],
        out_specs=jax.tree.map(lambda _: pl.BlockSpec(memory_space=pltpu.VMEM), out_shape),
        scratch_shapes=list(scratch),
        cost_estimate=pl.CostEstimate(flops=flops, bytes_accessed=flops // 512, transcendentals=0),
        compiler_params=pltpu.CompilerParams(vmem_limit_bytes=limit),
    )


def slot_spots(ids):
    expert = lax.broadcasted_iota(jnp.int32, (TOK, EXPERTS), 1)
    first = jnp.where(expert == ids[:, 0:1], 1.0, 0.0)
    second = jnp.where(expert == ids[:, 1:2], 1.0, 0.0)
    row = lax.broadcasted_iota(jnp.int32, (TOK, TOK), 0)
    col = lax.broadcasted_iota(jnp.int32, (TOK, TOK), 1)
    lower = jnp.where(row > col, 1.0, 0.0).astype(BF16)
    earlier = jnp.dot(lower, (first + second).astype(BF16), preferred_element_type=F32)
    base = CAP * expert.astype(F32) + earlier
    spot_first = jnp.sum(first * base, axis=-1, keepdims=True)
    spot_second = jnp.sum(second * base, axis=-1, keepdims=True)
    return first, second, spot_first, spot_second


def chunk_of(z, y):
    return lax.rem(z - y + 8, 8)


def holder_of(chunk, y):
    return lax.rem(chunk + y, 8)


def pack_kernel(
    mask_ref, query_hbm, key_hbm, value_hbm, residual_hbm, ids_hbm, out_ref, mask_out_ref,
    query_ref, key_ref, value_ref, residual_ref, ids_ref, sems,
):
    pairs = (
        (ids_hbm, ids_ref), (query_hbm, query_ref), (key_hbm, key_ref), (value_hbm, value_ref),
        (residual_hbm, residual_ref),
    )
    copies = [pltpu.make_async_copy(a, b, sems.at[i]) for i, (a, b) in enumerate(pairs)]
    for copy in copies:
        copy.start()
    z, y = lax.axis_index("z"), lax.axis_index("y")
    mask_out_ref[...] = mask_ref[...]
    copies[0].wait()
    expert = lax.broadcasted_iota(jnp.int32, (EXPERTS, TOK), 0)
    first = jnp.where(expert == ids_ref[0:1], 1.0, 0.0)
    second = jnp.where(expert == ids_ref[1:2], 1.0, 0.0)
    row = lax.broadcasted_iota(jnp.int32, (TOK, TOK), 0)
    col = lax.broadcasted_iota(jnp.int32, (TOK, TOK), 1)
    upper = jnp.where(row < col, 1.0, 0.0).astype(BF16)
    earlier = jnp.dot((first + second).astype(BF16), upper, preferred_element_type=F32)
    base = CAP * expert.astype(F32) + earlier
    spot_first = jnp.sum(first * base, axis=0, keepdims=True)
    spot_second = jnp.sum(second * base, axis=0, keepdims=True)
    row = lax.broadcasted_iota(jnp.int32, (16, TOK), 0)
    tile = jnp.where(row < 2, spot_first, jnp.where(row < 4, spot_second, 0.0)).astype(BF16)
    lane = lax.broadcasted_iota(jnp.int32, (TOK, 2 * HEAD), 1)
    token = lax.broadcasted_iota(jnp.int32, (TOK, 2 * HEAD), 0)
    here = jnp.where(lane == z * TOK + token, 1.0, 0.0).astype(BF16)
    tile = jnp.dot(tile, here, preferred_element_type=F32)
    row = lax.broadcasted_iota(jnp.int32, (16, HEAD), 0)
    tile = jnp.where(row % 2 == 0, tile[:, :HEAD], tile[:, HEAD:]).astype(BF16)
    for copy in copies[1:]:
        copy.wait()
    for h in range(8):
        cols = slice(h * HEAD, (h + 1) * HEAD)
        out_ref[h, 0:32] = query_ref[:, cols]
        out_ref[h, 32:64] = key_ref[:, cols]
        out_ref[h, 64:96] = value_ref[:, cols]
        out_ref[h, 160:176] = tile
        holder = holder_of(h, y)
        out_ref[holder, 96:128] = residual_ref[:, h * CHUNK : h * CHUNK + HEAD]
        out_ref[holder, 128:160] = residual_ref[:, h * CHUNK + HEAD : (h + 1) * CHUNK]


def spread_kernel(packed_ref, _, out_ref):
    for i in range(4):
        out_ref[i] = packed_ref[:, 32:96]


def attend_kernel(mask_ref, packed_ref, own_ref, other_ref, out_ref):
    x, c = lax.axis_index("x"), lax.axis_index("c")
    refs = (own_ref, other_ref)
    n_key = 2 * own_ref.shape[0] * TOK
    keys = jnp.concatenate([ref[:, :TOK].reshape(n_key // 2, HEAD) for ref in refs], axis=0)
    values = jnp.concatenate([ref[:, TOK:].reshape(n_key // 2, HEAD) for ref in refs], axis=0)
    key_row = lax.broadcasted_iota(jnp.int32, (1, n_key), 1)
    key_x, key_z, key_t = key_row // 256 % 4, key_row // 32 % 8, key_row % 32
    key_c = jnp.where(key_row < n_key // 2, c, 1 - c)
    key_pos = key_x * 512 + key_z * 64 + key_c * 32 + key_t
    block_row = lax.broadcasted_iota(jnp.int32, (16, n_key), 0)
    key_onehot = (block_row == jnp.broadcast_to(key_pos // BLOCK, (16, n_key))).astype(BF16)
    row_i = lax.broadcasted_iota(jnp.int32, (16, 16), 0)
    col_i = lax.broadcasted_iota(jnp.int32, (16, 16), 1)
    live = ((mask_ref[...] > 0) | (row_i == col_i)).astype(BF16)
    seen = jnp.dot(live, key_onehot, preferred_element_type=F32)
    seen_row = lax.broadcasted_iota(jnp.int32, (16, n_key), 0)
    scale = HEAD ** (-0.5)
    mine = [
        jnp.sum(jnp.where(seen_row == x * 4 + j, seen, 0.0), axis=0, keepdims=True) for j in range(4)
    ]
    mine = jnp.concatenate([jnp.broadcast_to(m, (2 * TOK, n_key)) for m in mine], axis=0)
    rows = packed_ref[:, :TOK].reshape(8 * TOK, HEAD)
    row = lax.broadcasted_iota(jnp.int32, (8 * TOK, 1), 0)
    query_pos = x * 512 + row // 32 * 64 + c * 32 + row % 32
    allowed = (mine > 0.5) & (key_pos <= query_pos)
    scores = lax.dot_general(rows, keys, (((1,), (1,)), ((), ())), preferred_element_type=F32)
    scores = jnp.where(allowed, scores * scale, -1e30)
    top = jnp.max(scores, axis=-1, keepdims=True)
    weights = jnp.exp(scores - top)
    total = jnp.sum(weights, axis=-1, keepdims=True)
    update = jnp.dot(weights.astype(BF16), values, preferred_element_type=F32)
    attended = (update / total).astype(BF16)
    for z in range(8):
        out_ref[z] = attended


def route_kernel(packed_ref, out_ref):
    spots = jnp.sum(packed_ref[:, 160:176].astype(F32), axis=0)
    spot_first = jnp.concatenate([spots[0:1], spots[1:2]], axis=1)
    spot_second = jnp.concatenate([spots[2:3], spots[3:4]], axis=1)
    row = lax.broadcasted_iota(jnp.int32, (8 * EXPERTS * CAP, 1), 0)
    row_spot = (row // 16 * CAP + row % CAP).astype(F32)
    row_block = row // CAP % 8
    col_block = lax.broadcasted_iota(jnp.int32, (1, 8 * TOK), 1) // TOK
    taken = (spot_first == row_spot) | (spot_second == row_spot)
    out_ref[...] = jnp.where(taken & (row_block == col_block), 1.0, 0.0).astype(BF16)


def project_kernel(
    att_ref, own_ref, core_ref, x_ref, x_core_ref, packed_ref, gain_ref, route_ref,
    attended_ref, projected_ref, buffer_ref,
):
    z, y = lax.axis_index("z"), lax.axis_index("y")
    mine = pl.ds(pl.multiple_of(z * TOK, TOK), TOK)
    attended_ref[...] = jnp.concatenate([att_ref[h, mine] for h in range(8)], axis=1)
    quarter = lax.axis_index("x") % 2 * 2 + lax.axis_index("c")
    total = None
    for ref, flip in ((own_ref, 0), (core_ref, 1), (x_ref, 2), (x_core_ref, 3)):
        rows = quarter ^ flip
        attended = jnp.concatenate([att_ref[2 * rows], att_ref[2 * rows + 1]], axis=1)
        part = jnp.dot(attended, ref[...], preferred_element_type=F32)
        total = part if total is None else total + part
    projected = total.astype(BF16)
    projected_ref[...] = projected.reshape(8, TOK, CHUNK)
    residual = jnp.concatenate(
        [packed_ref[:, 96:128].reshape(8 * TOK, HEAD), packed_ref[:, 128:160].reshape(8 * TOK, HEAD)],
        axis=1,
    )
    hidden = residual.astype(F32) + projected.astype(F32)
    scaled = (hidden * gain_ref[pl.ds(chunk_of(z, y), 1), :]).astype(BF16)
    rows = jnp.dot(route_ref[...], scaled, preferred_element_type=F32).astype(BF16)
    buffer_ref[...] = rows.reshape(EXPERTS, 16, CHUNK)


def gates_kernel(
    projected_ref, residual_ref, gain_ref, router_ref, ids_ref, down_hbm,
    hidden_ref, gates_ref, first_ref, second_ref, down_ref, sem,
):
    copy = pltpu.make_async_copy(down_hbm, down_ref, sem)
    copy.start()
    y = lax.axis_index("y")
    projected = jnp.concatenate([projected_ref[holder_of(k, y)] for k in range(8)], axis=1)
    hidden = residual_ref[...].astype(F32) + projected.astype(F32)
    hidden_ref[...] = hidden
    meansq = jnp.mean(hidden * hidden, axis=-1, keepdims=True)
    normed = (hidden * lax.rsqrt(meansq + 1e-06) * gain_ref[...]).astype(BF16)
    logits = jnp.dot(normed, router_ref[...], preferred_element_type=F32)
    first, second, spot_first, spot_second = slot_spots(ids_ref[...])
    logit_first = jnp.sum(first * logits, axis=-1, keepdims=True)
    logit_second = jnp.sum(second * logits, axis=-1, keepdims=True)
    gate = jax.nn.sigmoid(logit_first - logit_second)
    gates_ref[...] = jnp.concatenate([gate, 1.0 - gate], axis=1)
    spot = lax.broadcasted_iota(jnp.int32, (TOK, EXPERTS * CAP), 1).astype(F32)
    first_ref[...] = jnp.where(spot == spot_first, 1.0, 0.0).astype(BF16)
    second_ref[...] = jnp.where(spot == spot_second, 1.0, 0.0).astype(BF16)
    copy.wait()


def expert_kernel(rows_ref, inverse_ref, weight_ref, _, out_ref):
    transposed = (((1,), (1,)), ((), ()))
    streams = rows_ref.shape[0]
    first_stream = pl.program_id(0) * streams
    units = squares = None
    for k in range(8):
        piece = jnp.concatenate(
            [
                rows_ref[s, :, holder_of(k, first_stream + s)].reshape(128, CHUNK)
                for s in range(streams)
            ],
            axis=0,
        )
        plain = piece.astype(F32) * inverse_ref[k : k + 1, :]
        weight = weight_ref[:, k * CHUNK : (k + 1) * CHUNK]
        part = lax.dot_general(weight, piece, transposed, preferred_element_type=F32)
        units = part if k == 0 else units + part
        squares = plain * plain if k == 0 else squares + plain * plain
    high = squares.astype(BF16)
    low = (squares - high.astype(F32)).astype(BF16)
    ones = jnp.ones((16, CHUNK), BF16)
    sums = [lax.dot_general(ones, a, transposed, preferred_element_type=F32) for a in (high, low)]
    factor = lax.rsqrt((sums[0] + sums[1])[0:1] * (1.0 / D) + 1e-06)
    units = units * factor
    width = units.shape[0] // 2
    gate, up = units[:width], units[width:]
    active = (gate / (1.0 + jnp.exp(-gate)) * up).astype(BF16)
    for s in range(streams):
        out_ref[s] = active[:, s * 128 : (s + 1) * 128]


def expert_call(rows, inverse, weight, after):
    step = 4
    width = weight.shape[0] // 2
    whole = pl.BlockSpec(memory_space=pltpu.VMEM)
    return pl.pallas_call(
        expert_kernel,
        grid=(8 // step,),
        in_specs=[
            pl.BlockSpec((step, 4, 8, 2, 16, CHUNK), lambda i: (i, 0, 0, 0, 0, 0)),
            whole,
            whole,
            pl.BlockSpec(memory_space=pl.ANY),
        ],
        out_specs=pl.BlockSpec((step, width, 128), lambda i: (i, 0, 0)),
        out_shape=jax.ShapeDtypeStruct((8, width, 128), BF16),
        compiler_params=pltpu.CompilerParams(vmem_limit_bytes=51 * 1024 * 1024),
    )(rows, inverse, weight, after)


def down_kernel(active_ref, down_ref, out_ref):
    row = lax.broadcasted_iota(jnp.int32, (128, 128), 0)
    col = lax.broadcasted_iota(jnp.int32, (128, 128), 1)
    source = row // 32 * 32 + row // 2 % 2 * 16 + row // 4 % 8 * 2 + row % 2
    order = jnp.where(col == source, 1.0, 0.0).astype(BF16)
    hidden = active_ref.shape[0] * active_ref.shape[1]
    active = lax.dot_general(
        order,
        active_ref[...].reshape(hidden, 128),
        (((1,), (1,)), ((), ())),
        preferred_element_type=F32,
    ).astype(BF16)
    for k in range(4):
        cols = slice(k * 512, (k + 1) * 512)
        down = down_ref[:, :, cols].reshape(hidden, 512)
        out_ref[:, cols] = jnp.dot(active, down, preferred_element_type=F32).astype(BF16)


def combine_kernel(hidden_ref, gates_ref, first_ref, second_ref, rows_ref, out_ref):
    rows = rows_ref[...]
    first = jnp.dot(first_ref[...], rows, preferred_element_type=F32)
    second = jnp.dot(second_ref[...], rows, preferred_element_type=F32)
    moe = first * gates_ref[:, 0:1] + second * gates_ref[:, 1:2]
    out_ref[...] = (hidden_ref[...] + moe).astype(BF16)


def shards(
    residual,
    queries,
    keys,
    values,
    block_mask,
    out_weight,
    norm_gain,
    router,
    route_ids,
    w_gate,
    w_up,
    w_down,
):
    seq = ("x", "z", "c")
    ids = route_ids[0]
    shape = lambda *s: jax.ShapeDtypeStruct(s, BF16)
    swap = lambda a, axes: lax.all_to_all(a, axes, split_axis=0, concat_axis=0, tiled=True)

    down = lax.all_gather(w_down[0], "y", axis=0)
    share = out_weight.shape[0] // 4
    quarter = lax.axis_index("x") % 2 * 2 + lax.axis_index("c")
    weight = lax.dynamic_slice_in_dim(out_weight, quarter * share, share, axis=0)
    weight = lax.ppermute(
        weight, ("z", "y"), [(z * 8 + y, z * 8 + (z - y) % 8) for z in range(8) for y in range(8)]
    )

    packed, mask = vmem_call(
        pack_kernel,
        (shape(8, 176, HEAD), jax.ShapeDtypeStruct(block_mask.shape[1:], jnp.int32)),
        6,
        hbm=(1, 2, 3, 4, 5),
        scratch=(
            *(pltpu.VMEM((TOK, 8 * HEAD), BF16) for _ in range(3)),
            pltpu.VMEM((TOK, D), BF16),
            pltpu.VMEM((2, TOK), jnp.int32),
            pltpu.SemaphoreType.DMA((5,)),
        ),
        limit=60 * 1024 * 1024,
    )(block_mask[0], queries[0], keys[0], values[0], residual[0], ids.T)
    packed = swap(packed, "z")
    other_core = [(0, 1), (1, 0)]
    kv = vmem_call(spread_kernel, shape(4, 8, 2 * TOK, HEAD), 2, unread=(1,))(packed, weight)
    kv = swap(kv, "x").reshape(32, 2 * TOK, HEAD)
    other_kv = lax.ppermute(kv, "c", other_core)
    att = vmem_call(attend_kernel, shape(8, 8 * TOK, HEAD), 4)(mask, packed, kv, other_kv)
    beside = lax.ppermute(weight, "x", [(0, 1), (1, 0), (2, 3), (3, 2)])
    weights = (
        weight, lax.ppermute(weight, "c", other_core), beside, lax.ppermute(beside, "c", other_core)
    )
    att = swap(att, "z")
    route = vmem_call(route_kernel, shape(8 * EXPERTS * CAP, 8 * TOK), 1, flops=2_000_000_000)(packed)
    attended, projected, buffer = vmem_call(
        project_kernel,
        (shape(TOK, 8 * HEAD), shape(8, TOK, CHUNK), shape(EXPERTS, 16, CHUNK)),
        8,
    )(att, *weights, packed, norm_gain.reshape(8, CHUNK), route)

    arrived = swap(buffer, seq) + down[0, 0, 0] * 0
    rows = lax.all_gather(arrived, "y", axis=0)
    projected = swap(projected, "z")
    hidden, gates, first, second, down = vmem_call(
        gates_kernel,
        (
            jax.ShapeDtypeStruct((TOK, D), F32),
            jax.ShapeDtypeStruct((TOK, 2), F32),
            shape(TOK, EXPERTS * CAP),
            shape(TOK, EXPERTS * CAP),
            shape(*down.shape),
        ),
        6,
        hbm=(5,),
        scratch=(pltpu.SemaphoreType.DMA(()),),
    )(projected, residual[0], norm_gain[None], router, ids, down)

    active = expert_call(
        rows.reshape(8, 4, 8, 2, 16, CHUNK),
        (1.0 / norm_gain).reshape(8, CHUNK),
        jnp.concatenate([w_gate[0].T, w_up[0].T], axis=0),
        gates,
    )
    out = vmem_call(down_kernel, shape(128, D), 2)(swap(active, "y"), down)
    returned = swap(out.reshape(EXPERTS, CAP, D), seq)
    mixed = vmem_call(combine_kernel, shape(TOK, D), 5)(
        hidden, gates, first, second, returned.reshape(EXPERTS * CAP, D)
    )
    return (attended[None], mixed[None])


def solution(mesh):
    mesh = Mesh(mesh.devices.reshape(4, 8, 2, 8), ("x", "z", "c", "y"))
    seq = ("x", "z", "c")
    placed = (
        P("y", seq, None),
        P("y", seq, None),
        P("y", seq, None),
        P("y", seq, None),
        P("y", None, None),
        P(None, "y"),
        P(),
        P(),
        P("y", seq, None),
        P(seq, None, "y"),
        P(seq, None, "y"),
        P(seq, "y", None),
    )
    return jax.shard_map(
        shards,
        mesh=mesh,
        in_specs=placed,
        out_specs=(P("y", seq, None), P("y", seq, None)),
        check_vma=False,
    )
```
